32 devices in a mesh: dp: 8 (over z, x), tensor: 4 (over y, core).
Axes of the slice: x: 2, y: 2, z: 4, core: 2. Of those that a mesh axis runs over, the one named last changes fastest.
Arguments:
- hidden_first: bfloat16 [1024, 2048], P('dp', 'tensor'), may hold values from -6 to 6
- hidden_second: bfloat16 [1024, 2048], P('dp', 'tensor'), may hold values from -6 to 6
- cotangent: bfloat16 [1024, 2048], P('dp', 'tensor'), may hold values from -6 to 6
- depths: int32 [1024], P('dp'), may hold values from 0 to 2, as said below
- norm_gain: float32 [2048], replicated, may hold values from 0.5 to 1.5
- router: float32 [2, 2048], replicated, may hold values from -0.125 to 0.125
- w_gate: bfloat16 [2048, 4096], P(None, 'tensor'), may hold values from -0.125 to 0.125
- w_up: bfloat16 [2048, 4096], P(None, 'tensor'), may hold values from -0.125 to 0.125
- w_down: bfloat16 [4096, 2048], P('tensor'), may hold values from -0.09375 to 0.09375
Outputs:
- grad_first: bfloat16 [1024, 2048], P('dp', 'tensor')
The draws below stay inside these ranges and needn't reach their ends.
Inputs may be any that keep to these rules, and one draw needn't show every extreme that they name: `depths`: exactly 512 tokens have depth 1 or more and exactly 256 have depth 2; the active tokens are unevenly spread over the tokens of one dp index.
All inputs are finite; a program needn't handle non-finite values.
Results may differ from the reference program's by a relative error of at most 0.02.
Values may be sent and summed in bfloat16 or wider, within the bound.
No kernel may reach another device: no remote copies, remote signals or barrier semaphores. Data moves between devices by JAX's collectives and lax.ppermute only.
A program may use at most 64 MiB of HBM per device.

```python
import jax
import jax.numpy as jnp
from jax import lax

D = 2048
FF = 4096
TOK_DEV = 128
TOKENS = 1024


def draw_depths(key, part):
    key = jax.random.fold_in(key, 11)
    block_key, noise_key = jax.random.split(key)
    block_count = TOKENS // TOK_DEV
    block_weight = jax.random.randint(block_key, (block_count,), 0, 4)
    noise_draw = jax.random.randint(noise_key, (TOKENS,), 0, 1024)
    token_score = (noise_draw + jnp.repeat(block_weight, TOK_DEV) * 512) * TOKENS + jnp.arange(TOKENS)
    sort_order = jnp.argsort(-token_score, stable=True)
    token_rank = jnp.argsort(sort_order, stable=True)
    return jnp.where(token_rank < TOKENS // 4, 2, jnp.where(token_rank < TOKENS // 2, 1, 0)).astype(jnp.int32)


def levels(own_key, extent, pieces, smallest, largest):
    loudness = 1.0
    for position, blocks in pieces:
        steps = jax.random.uniform(jax.random.fold_in(jax.random.fold_in(own_key, 6), position), (blocks,), jnp.float32, smallest / len(pieces), largest / len(pieces))
        loudness = loudness * jnp.repeat(jnp.exp(steps), extent[position] // blocks).reshape((-1,) + (1,) * (len(extent) - 1 - position))
    return loudness


def scatter_about(stream_key, extent, width, bound, shards=(), held_as=jnp.bfloat16):
    result = jax.random.normal(stream_key, extent, jnp.float32) * width
    if len(shards) > 0:
        result = levels(stream_key, extent, shards, -0.22, 0.18) * result
    return jnp.clip(result, min=-bound, max=bound).astype(held_as)


def setup_inputs(seed: int = 0) -> dict:
    splits = jax.random.split(jax.random.key(seed), 10)
    return {
        "hidden_first": scatter_about(splits[0], (TOKENS, D), 1.0, 6.0, ((0, 8), (1, 4))),
        "hidden_second": scatter_about(splits[1], (TOKENS, D), 1.0, 6.0, ((0, 8), (1, 4))),
        "cotangent": scatter_about(splits[2], (TOKENS, D), 1.0, 6.0, ((0, 8), (1, 4))),
        "depths": draw_depths(jax.random.fold_in(splits[9], 71), 0),
        "norm_gain": jnp.clip(1.0 + 0.1 * jax.random.normal(splits[4], (D,), jnp.float32), 0.5, 1.5),
        "router": scatter_about(splits[5], (2, D), D ** -0.5, 0.125, (), jnp.float32),
        "w_gate": scatter_about(splits[6], (D, FF), D ** -0.5, 0.125, ((1, 4),)),
        "w_up": scatter_about(splits[7], (D, FF), D ** -0.5, 0.125, ((1, 4),)),
        "w_down": scatter_about(splits[8], (FF, D), FF ** -0.5, 0.09375, ((0, 4),)),
    }


epsilon = 1e-06

def block_grad(rows, cot_rows, router_row, norm_gain, w_gate, w_up, w_down):
    x_float = rows.astype(jnp.float32)
    wide = rows.shape[1]
    inv_rms = lax.rsqrt(lax.optimization_barrier(jnp.mean(x_float * x_float, axis=1, keepdims=True)) + epsilon)
    normed = (x_float * inv_rms * norm_gain).astype(jnp.bfloat16)
    gate_pre = jnp.dot(normed, w_gate, preferred_element_type=jnp.float32)
    up_pre = jnp.dot(normed, w_up, preferred_element_type=jnp.float32)
    sigma = jax.nn.sigmoid(gate_pre)
    silu_val = gate_pre * sigma
    hidden_act = (silu_val * up_pre).astype(jnp.bfloat16)
    score = jax.nn.sigmoid(jnp.dot(x_float, router_row, precision=lax.Precision.HIGHEST))
    back_hidden = jnp.dot(cot_rows, w_down.T, preferred_element_type=jnp.float32)
    score_grad = lax.optimization_barrier(jnp.sum(hidden_act.astype(jnp.float32) * back_hidden, axis=1))
    scaled = score[:, None] * back_hidden
    grad_gate = (scaled * up_pre * sigma * (1.0 + gate_pre * (1.0 - sigma))).astype(jnp.bfloat16)
    grad_up = (scaled * silu_val).astype(jnp.bfloat16)
    grad_norm = jnp.dot(grad_gate, w_gate.T, preferred_element_type=jnp.float32) + jnp.dot(grad_up, w_up.T, preferred_element_type=jnp.float32)
    scaled_grad = grad_norm * norm_gain
    row_dot = lax.optimization_barrier(jnp.sum(x_float * scaled_grad, axis=1))
    logit_grad = score_grad * score * (1.0 - score)
    delta = inv_rms * scaled_grad - x_float * inv_rms ** 3 * (row_dot / wide)[:, None] + logit_grad[:, None] * router_row[None, :]
    return (cot_rows.astype(jnp.float32) + delta).astype(jnp.bfloat16)

def recursion(rows_all, cot_all, active, count, router_row, norm_gain, w_gate, w_up, w_down):
    picked = jnp.nonzero(active, size=count)[0].astype(jnp.int32)
    grads = block_grad(rows_all[picked], cot_all[picked], router_row, norm_gain, w_gate, w_up, w_down)
    return cot_all.at[picked].set(grads)

def reference(hidden_first, hidden_second, cotangent, depths, norm_gain, router, w_gate, w_up, w_down):
    grad_second = recursion(hidden_second, cotangent, depths >= 2, TOKENS // 4, router[1], norm_gain, w_gate, w_up, w_down)
    return recursion(hidden_first, grad_second, depths >= 1, TOKENS // 2, router[0], norm_gain, w_gate, w_up, w_down)
```

```python
import functools

import jax
import jax.numpy as jnp
from jax import lax
from jax.experimental import pallas as pl
from jax.experimental.pallas import tpu as pltpu
from jax.sharding import PartitionSpec as P

epsilon = 1e-06
LANES = 128
EXTRA = 16
VM = pltpu.VMEM
F32 = jnp.float32
BF16 = jnp.bfloat16


def hop(value, bit):
    size = lax.axis_size("tensor")
    return lax.ppermute(value, "tensor", [(j, j ^ bit) for j in range(size)])


def after(value, *others):
    return lax.optimization_barrier((value,) + others)[0]


def spread(own, low_bits):
    parts = {0: own}
    for bit in reversed(low_bits):
        for key in list(parts):
            parts[key ^ bit] = hop(parts[key], bit)
    return [parts[key] for key in range(len(parts))]


def scatter(blocks, low_bits):
    blocks = dict(enumerate(blocks))
    for bit in low_bits:
        kept = {}
        for r in sorted(blocks):
            if r & bit == 0:
                kept[r] = blocks[r].astype(F32) + hop(blocks[r ^ bit].astype(BF16), bit).astype(F32)
        blocks = kept
    return blocks[0]


def kernel_call(kernel, outs, *args, flops=0):
    many = isinstance(outs, (list, tuple))
    shapes = outs if many else [outs]
    moved = sum(a.size * a.dtype.itemsize for a in args)
    spec = pl.BlockSpec(memory_space=VM)
    return pl.pallas_call(
        kernel,
        out_shape=list(outs) if many else outs,
        in_specs=[spec] * len(args),
        out_specs=[spec] * len(shapes) if many else spec,
        compiler_params=pltpu.CompilerParams(vmem_limit_bytes=16 * 2**20),
        cost_estimate=pl.CostEstimate(flops=flops, bytes_accessed=moved, transcendentals=0),
    )(*args)


def place(top):
    index = lax.axis_index("tensor")
    return index // top, index % top


def span(block, feat):
    return pl.ds(pl.multiple_of(block * feat, feat), feat)


def turned(value):
    value = value.astype(F32)
    return jnp.concatenate(
        [value[:, k : k + LANES].T for k in range(0, value.shape[1], LANES)], axis=0
    )


def column(row, tokens):
    return turned(jnp.broadcast_to(row, (tokens, row.shape[1])))


def mat(left, right):
    return jnp.dot(left, right, preferred_element_type=F32)


def turn_kernel(value_ref, out_ref):
    out_ref[...] = turned(value_ref[...]).astype(out_ref.dtype)


def norm_kernel(top, which, halves, router_row, first, last, *refs):
    refs = list(refs)
    parts = [refs.pop(0) for _ in halves for _ in range(top)]
    gain_ref, router_ref, gate_w, up_w = [refs.pop(0) for _ in range(4)]
    held = [] if first else [refs.pop(0) for _ in range(3)]
    outs = refs
    side, inner = place(top)
    feat = parts[0].shape[1]
    wide = feat * top * 2
    gate = up = None
    squares = jnp.zeros((parts[0].shape[0], LANES), F32)
    logits = jnp.zeros((parts[0].shape[0], LANES), F32)
    if not first:
        gate, up = held[0][...], held[1][...]
        squares, logits = held[2][0], held[2][1]
    for number, part in enumerate(parts):
        half = halves[number // top]
        block = (side if half == 0 else 1 - side) * top + (inner ^ (number % top))
        at = span(block, feat)
        x = part[...].astype(F32)
        gained = (x * gain_ref[:, at]).astype(BF16)
        routed = x * router_ref[router_row : router_row + 1, at]
        for k in range(0, feat, LANES):
            squares += x[:, k : k + LANES] * x[:, k : k + LANES]
            logits += routed[:, k : k + LANES]
        gate_now, up_now = mat(gained, gate_w[at, :]), mat(gained, up_w[at, :])
        gate = gate_now if gate is None else gate + gate_now
        up = up_now if up is None else up + up_now
    if not last:
        outs[0][...], outs[1][...] = gate, up
        outs[2][0], outs[2][1] = squares, logits
        return
    inv_rms = lax.rsqrt(jnp.sum(squares.T, axis=0, keepdims=True) / wide + epsilon)
    score = jax.nn.sigmoid(jnp.sum(logits.T, axis=0, keepdims=True))
    rows = outs[4]
    rows[...] = jnp.concatenate(
        [inv_rms, score, jnp.zeros((6, inv_rms.shape[1]), F32)], axis=0
    )
    for k in range(0, gate.shape[1], LANES):
        g = gate[:, k : k + LANES].T * inv_rms
        u = up[:, k : k + LANES].T * inv_rms
        sigma = jax.nn.sigmoid(g)
        silu = g * sigma
        grad = u * sigma * (1.0 + g * (1.0 - sigma))
        act = silu * u
        here = slice(k, k + LANES)
        outs[0][here, :] = score * grad
        outs[1][here, :] = score * silu
        outs[2][here, :] = act
        outs[3][here, :] = score * (grad * g + act)


def back_part_kernel(top, half, *refs):
    parts, (down_w, out_ref) = refs[:top], refs[top:]
    side, inner = place(top)
    feat = parts[0].shape[0]
    start = (side if half == "mine" else 1 - side if half == "theirs" else half) * top
    total = None
    for r, part in enumerate(parts):
        now = mat(down_w[:, span(start + (inner ^ r), feat)], part[...])
        total = now if total is None else total + now
    out_ref[...] = total


def write_terms(top, half, feat, gg, gu, sums, gate_w, up_w, outs):
    side, inner = place(top)
    start = (side if half == "mine" else 1 - side if half == "theirs" else half) * top
    for r, out_ref in enumerate(outs):
        at = span(start + (inner ^ r), feat)
        term = mat(gate_w[at, :], gg) + mat(up_w[at, :], gu)
        out_ref[0:feat, :] = term.astype(out_ref.dtype)
        out_ref[feat : feat + EXTRA, :] = sums.astype(out_ref.dtype)


def back_kernel(top, half, out_half, feat, *refs):
    parts = refs[:top]
    held, grad_p, silu_p, act_p, dot_p, down_w, gate_w, up_w, gg_ref, gu_ref, sums_ref = refs[
        top : top + 11
    ]
    outs = refs[top + 11 :]
    side, inner = place(top)
    start = (side if half == "mine" else 1 - side if half == "theirs" else half) * top
    back = held[...]
    for r, part in enumerate(parts):
        back = back + mat(down_w[:, span(start + (inner ^ r), feat)], part[...])
    gg = (back * grad_p[...]).astype(BF16)
    gu = (back * silu_p[...]).astype(BF16)
    score_part = jnp.sum(back * act_p[...], axis=0, keepdims=True)
    dot_part = jnp.sum(back * dot_p[...], axis=0, keepdims=True)
    sums = jnp.concatenate(
        [score_part, dot_part, jnp.zeros((EXTRA - 2, LANES), F32)], axis=0
    )
    gg_ref[...] = gg
    gu_ref[...] = gu
    sums_ref[...] = sums
    write_terms(top, out_half, feat, gg, gu, sums, gate_w, up_w, outs)


def term_kernel(top, half, feat, gg_ref, gu_ref, sums_ref, gate_w, up_w, *outs):
    write_terms(top, half, feat, gg_ref[...], gu_ref[...], sums_ref[...], gate_w, up_w, outs)


def row_factors(sums, rows, wide):
    inv_rms, score = rows[0:1, :], rows[1:2, :]
    return inv_rms, inv_rms * inv_rms * (sums[1:2, :] / wide), sums[0:1, :] * score * (1.0 - score)


def second_kernel(top, half, chip, got, cot_own, cot_cross, x_own, x_cross, gain_ref, router_ref, depths_ref, rows_ref, out_ref):
    side, inner = place(top)
    feat = out_ref.shape[0]
    tokens = x_own.shape[0]
    total = chip[...] + got[...].astype(F32)
    inv_rms, coef, logit = row_factors(total[feat : feat + 2, :], rows_ref[...], feat * top * 2)
    active = (depths_ref[...] >= 2).astype(F32)
    at = span(half * top + inner, feat)
    mine = side == half
    x = turned(jnp.where(mine, x_own[...].astype(F32), x_cross[...].astype(F32)))
    cot = jnp.where(mine, cot_own[...].astype(F32), cot_cross[...].astype(F32))
    gain = column(gain_ref[:, at], tokens)
    router = column(router_ref[1:2, at], tokens)
    delta = (active * inv_rms) * (gain * total[0:feat, :]) - x * (active * coef) + router * (active * logit)
    out_ref[...] = (cot + delta).astype(out_ref.dtype)


def last_kernel(top, own_sum, chip_theirs, got, second_a, second_b, x_own, gain_ref, router_ref, depths_ref, rows_ref, out_ref):
    side, inner = place(top)
    tokens, feat = out_ref.shape
    cross = got[...].astype(F32)
    total = own_sum[0:feat, :] + cross[0:feat, :]
    sums = chip_theirs[feat : feat + 2, :] + cross[feat : feat + 2, :]
    inv_rms, coef, logit = row_factors(sums, rows_ref[...], feat * top * 2)
    active = (depths_ref[...] >= 1).astype(F32)
    at = span(side * top + inner, feat)
    x = turned(x_own[...])
    gain = column(gain_ref[:, at], tokens)
    router = column(router_ref[0:1, at], tokens)
    second = jnp.where(side == 0, second_a[...].astype(F32), second_b[...].astype(F32))
    delta = (active * inv_rms) * (gain * total) - x * (active * coef) + router * (active * logit)
    result = second + delta
    for k in range(0, feat, LANES):
        out_ref[:, k : k + LANES] = result[k : k + LANES, :].T.astype(out_ref.dtype)


def body(hidden_first, hidden_second, cotangent, depths, norm_gain, router, w_gate, w_up, w_down):
    size = lax.axis_size("tensor")
    bits = []
    while 2 ** len(bits) < size:
        bits.append(2 ** len(bits))
    top, low = bits[-1], bits[:-1]
    tokens, feat = hidden_first.shape
    units = w_gate.shape[1]
    depths = depths.reshape(1, tokens)
    gain = norm_gain.reshape(1, -1)
    product = 2 * tokens * feat * top * units
    wide_units = VM((units, LANES), F32)
    factor_outs = [wide_units] * 4 + [VM((8, LANES), F32)]
    partial_outs = [VM((tokens, units), F32)] * 2 + [VM((2, tokens, LANES), F32)]
    block_outs = [VM((feat + EXTRA, LANES), BF16 if r & 1 else F32) for r in range(top)]
    grad_outs = [VM((units, LANES), BF16)] * 2 + [VM((EXTRA, LANES), F32)]

    x2_cross = hop(hidden_second, top)
    x2_mine = spread(hidden_second, low)
    cot_own = kernel_call(turn_kernel, VM((feat, tokens), BF16), cotangent)
    cot_cross = hop(cot_own, top)
    cot_mine = spread(cot_own, low)
    x2_theirs = spread(x2_cross, low)
    norm_weights = (gain, router, w_gate, w_up)
    partial = kernel_call(
        functools.partial(norm_kernel, top, "a", (0,), 1, True, False),
        partial_outs, *x2_mine, *norm_weights, flops=2 * product,
    )
    back_mine = kernel_call(
        functools.partial(back_part_kernel, top, "mine"),
        wide_units, *cot_mine, w_down, flops=product,
    )
    factors2 = kernel_call(
        functools.partial(norm_kernel, top, "b", (1,), 1, False, True),
        factor_outs, *x2_theirs, *norm_weights, *partial, flops=2 * product,
    )
    cot_theirs = spread(cot_cross, low)

    gg, gu, sums, *blocks = kernel_call(
        functools.partial(back_kernel, top, "theirs", 0, feat),
        grad_outs + block_outs,
        *cot_theirs, back_mine, *factors2[:4], w_down, w_gate, w_up, flops=3 * product,
    )
    chip_a = scatter(blocks, low)
    blocks = kernel_call(
        functools.partial(term_kernel, top, 1, feat),
        block_outs, gg, gu, sums, w_gate, w_up, flops=2 * product,
    )
    got_a = hop(chip_a.astype(BF16), top)
    chip_b = scatter(blocks, low)
    got_b = hop(chip_b.astype(BF16), top)

    x1_cross = hop(after(hidden_first, cot_cross), top)
    x1_parts = spread(hidden_first, low) + spread(x1_cross, low)
    x1_parts = list(lax.optimization_barrier((tuple(x1_parts), chip_b))[0])
    factors1 = kernel_call(
        functools.partial(norm_kernel, top, "c", (0, 1), 0, True, True),
        factor_outs, *x1_parts, *norm_weights, flops=4 * product,
    )

    seconds = []
    for half, chip, got in ((0, chip_a, got_a), (1, chip_b, got_b)):
        seconds.append(
            kernel_call(
                functools.partial(second_kernel, top, half),
                VM((feat, tokens), BF16),
                chip, got, cot_own, cot_cross, hidden_second, x2_cross, gain, router, depths,
                factors2[4],
            )
        )
    second_a, second_b = (spread(value, low) for value in seconds)
    back_a = kernel_call(
        functools.partial(back_part_kernel, top, 0), wide_units, *second_a, w_down, flops=product
    )
    gg, gu, sums, *blocks = kernel_call(
        functools.partial(back_kernel, top, 1, "theirs", feat),
        grad_outs + block_outs,
        *second_b, back_a, *factors1[:4], w_down, w_gate, w_up, flops=3 * product,
    )
    chip_theirs = scatter(blocks, low)
    got = hop(chip_theirs.astype(BF16), top)
    blocks = kernel_call(
        functools.partial(term_kernel, top, "mine", feat),
        block_outs, gg, gu, sums, w_gate, w_up, flops=2 * product,
    )
    own_sum = scatter(blocks, low)
    return kernel_call(
        functools.partial(last_kernel, top),
        jax.ShapeDtypeStruct((tokens, feat), BF16),
        own_sum, chip_theirs, got, seconds[0], seconds[1], hidden_first, gain, router, depths,
        factors1[4],
    )


def solution(mesh):
    in_specs = (
        P("dp", "tensor"),
        P("dp", "tensor"),
        P("dp", "tensor"),
        P("dp"),
        P(),
        P(),
        P(None, "tensor"),
        P(None, "tensor"),
        P("tensor", None),
    )
    out_specs = P("dp", "tensor")
    return jax.shard_map(body, mesh=mesh, in_specs=in_specs, out_specs=out_specs, check_vma=False)
```

```python
import functools

import jax
import jax.numpy as jnp
from jax import lax
from jax.experimental import pallas as pl
from jax.experimental.pallas import tpu as pltpu
from jax.sharding import PartitionSpec as P

epsilon = 1e-06
LANES = 128
EXTRA = 16
PIECE = 256
VM = pltpu.VMEM
F32 = jnp.float32
BF16 = jnp.bfloat16


def hop(value, bit):
    size = lax.axis_size("tensor")
    return lax.ppermute(value, "tensor", [(j, j ^ bit) for j in range(size)])


def after(value, *others):
    return lax.optimization_barrier((value,) + others)[0]


def spread(own, low_bits):
    parts = {0: own}
    for bit in reversed(low_bits):
        for key in list(parts):
            parts[key ^ bit] = hop(parts[key], bit)
    return [parts[key] for key in range(len(parts))]


def kernel_call(kernel, outs, *args, flops=0, far=(), scratch=()):
    many = isinstance(outs, (list, tuple))
    args = [
        pltpu.with_memory_space_constraint(a, pltpu.HBM) if n in far else a
        for n, a in enumerate(args)
    ]
    near = pl.BlockSpec(memory_space=VM)
    away = pl.BlockSpec(memory_space=pltpu.HBM)
    return pl.pallas_call(
        kernel,
        out_shape=list(outs) if many else outs,
        in_specs=[away if n in far else near for n in range(len(args))],
        out_specs=[near] * len(outs) if many else near,
        scratch_shapes=list(scratch),
        compiler_params=pltpu.CompilerParams(vmem_limit_bytes=8 * 2**20),
        cost_estimate=pl.CostEstimate(flops=flops, bytes_accessed=0, transcendentals=0),
    )(*args)


def place(top):
    index = lax.axis_index("tensor")
    return index // top, index % top


def span(block, feat):
    return pl.ds(pl.multiple_of(block * feat, feat), feat)


def inside(top, key, feat):
    return span(place(top)[1] ^ (key % top), feat)


def overall(top, key, feat):
    side, inner = place(top)
    return span((side * top + inner) ^ key, feat)


def turned(value):
    value = value.astype(F32)
    return jnp.concatenate(
        [value[:, k : k + LANES].T for k in range(0, value.shape[1], LANES)], axis=0
    )


def column(row, tokens):
    return turned(jnp.broadcast_to(row, (tokens, row.shape[1])))


def mat(left, right):
    return jnp.dot(left, right, preferred_element_type=F32)


def mat_turned(left, right):
    return lax.dot_general(
        left, right, (((1,), (1,)), ((), ())), preferred_element_type=F32
    )


def fetch(sems, pairs):
    copies = []
    for n, (source, target) in enumerate(pairs):
        copy = pltpu.make_async_copy(source, target, sems.at[n])
        copy.start()
        copies.append(copy)
    return copies


def pieces(source, target):
    rows = target.shape[0]
    step = min(PIECE, rows)
    return [
        (source.at[n : n + step, :], target.at[n : n + step, :]) for n in range(0, rows, step)
    ]


def half_rows(top, far, mine):
    half = far.shape[0] // 2
    side, _ = place(top)
    return far.at[span(side if mine else 1 - side, half), :]


def norm_block(top, key, x_ref, router_row, gain_ref, router_ref, gate_w, up_w, total):
    gate, up, squares, logits = total
    feat = x_ref.shape[1]
    at, rows = overall(top, key, feat), inside(top, key, feat)
    x = x_ref[...].astype(F32)
    gained = (x * gain_ref[:, at]).astype(BF16)
    routed = x * router_ref[router_row : router_row + 1, at]
    for k in range(0, feat, LANES):
        squares = squares + x[:, k : k + LANES] * x[:, k : k + LANES]
        logits = logits + routed[:, k : k + LANES]
    gate_now, up_now = mat(gained, gate_w[rows, :]), mat(gained, up_w[rows, :])
    if gate is None:
        return gate_now, up_now, squares, logits
    return gate + gate_now, up + up_now, squares, logits


def norm_start(tokens):
    zeros = jnp.zeros((tokens, LANES), F32)
    return None, None, zeros, zeros


def own_kernel(top, router_row, *refs):
    smalls, (gate_far, up_far, down_far), small_outs, nears, outs, sems = (
        refs[:6], refs[6:9], refs[9:15], refs[15:18], refs[18:22], refs[22]
    )
    copies = fetch(
        sems,
        [
            *zip(smalls, small_outs),
            *pieces(half_rows(top, gate_far, True), nears[0]),
            *pieces(half_rows(top, up_far, True), nears[1]),
            *pieces(down_far, nears[2]),
        ],
    )
    ready = 6 + 2 * len(pieces(nears[0], nears[0]))
    for copy in copies[:ready]:
        copy.wait()
    x, cot, _, gain_ref, router_ref, _ = small_outs
    total = norm_block(
        top, 0, x, router_row, gain_ref, router_ref, *nears[:2], norm_start(x.shape[0])
    )
    outs[0][...], outs[1][...], outs[2][0], outs[2][1] = total
    for copy in copies[ready:]:
        copy.wait()
    outs[3][...] = back_raw(top, (0,), (cot,), nears[2])


def near_kernel(top, router_row, *refs):
    n = top - 1
    xs, cots, weights, down_w, held, fars, outs, nears, sems = (
        refs[:n], refs[n : 2 * n], refs[2 * n : 2 * n + 4], refs[2 * n + 4],
        refs[2 * n + 5 : 2 * n + 9], refs[2 * n + 9 : 2 * n + 11],
        refs[2 * n + 11 : 2 * n + 15], refs[2 * n + 15 : 2 * n + 17], refs[2 * n + 17],
    )
    copies = fetch(
        sems,
        [pair for far, near in zip(fars, nears) for pair in pieces(half_rows(top, far, False), near)],
    )
    total = (held[0][...], held[1][...], held[2][0], held[2][1])
    for key, x in enumerate(xs):
        total = norm_block(top, key + 1, x, router_row, *weights, total)
    outs[0][...], outs[1][...], outs[2][0], outs[2][1] = total
    outs[3][...] = back_raw(top, range(1, top), cots, down_w, held[3][...])
    for copy in copies:
        copy.wait()


def write_factors(total, wide, outs):
    gate, up, squares, logits = total
    inv_rms = lax.rsqrt(jnp.sum(squares.T, axis=0, keepdims=True) / wide + epsilon)
    score = jax.nn.sigmoid(jnp.sum(logits.T, axis=0, keepdims=True))
    outs[4][...] = jnp.concatenate(
        [inv_rms, score, jnp.zeros((6, inv_rms.shape[1]), F32)], axis=0
    )
    for k in range(0, gate.shape[1], LANES):
        g = gate[:, k : k + LANES].T * inv_rms
        u = up[:, k : k + LANES].T * inv_rms
        sigma = jax.nn.sigmoid(g)
        silu = g * sigma
        grad = u * sigma * (1.0 + g * (1.0 - sigma))
        act = silu * u
        here = slice(k, k + LANES)
        outs[0][here, :] = score * grad
        outs[1][here, :] = score * silu
        outs[2][here, :] = act
        outs[3][here, :] = score * (grad * g + act)


def factors_second_kernel(top, router_row, *refs):
    xs, (gain_ref, router_ref, gate_w, up_w), held, outs = (
        refs[:top], refs[top : top + 4], refs[top + 4 : top + 7], refs[top + 7 :]
    )
    total = (held[0][...], held[1][...], held[2][0], held[2][1])
    for n, x in enumerate(xs):
        total = norm_block(top, top + n, x, router_row, gain_ref, router_ref, gate_w, up_w, total)
    write_factors(total, gain_ref.shape[1], outs)


def factors_first_kernel(top, router_row, *refs):
    xs, (gain_ref, router_ref), weights, outs = (
        refs[: 2 * top], refs[2 * top : 2 * top + 2], refs[2 * top + 2 : 2 * top + 6],
        refs[2 * top + 6 :],
    )
    total = norm_start(xs[0].shape[0])
    for key, x in enumerate(xs):
        gate_w, up_w = weights[:2] if key < top else weights[2:]
        total = norm_block(top, key, x, router_row, gain_ref, router_ref, gate_w, up_w, total)
    write_factors(total, gain_ref.shape[1], outs)


def back_raw(top, keys, parts, down_w, total=None):
    for key, part in zip(keys, parts):
        now = mat_turned(down_w[:, overall(top, key, part.shape[1])], part[...])
        total = now if total is None else total + now
    return total


def back_sum(top, keys, parts, down_w, total=None):
    for key, part in zip(keys, parts):
        now = mat(down_w[:, overall(top, key, part.shape[0])], part[...])
        total = now if total is None else total + now
    return total


def back_part_kernel(top, keys, *refs):
    n = len(keys)
    refs[n + 1][...] = back_sum(top, keys, refs[:n], refs[n])


def write_terms(top, keys, gg, gu, sums, weights, outs):
    for n, out_ref in enumerate(outs):
        gate_w, up_w = weights[2 * (n // len(keys)) : 2 * (n // len(keys)) + 2]
        feat = out_ref.shape[0] - EXTRA
        rows = inside(top, keys[n % len(keys)], feat)
        term = mat(gate_w[rows, :], gg) + mat(up_w[rows, :], gu)
        out_ref[0:feat, :] = term.astype(out_ref.dtype)
        out_ref[feat : feat + EXTRA, :] = sums.astype(out_ref.dtype)


def double(out_ref):
    rows = out_ref.shape[0] // 2
    return out_ref.at[0:rows, :], out_ref.at[rows : 2 * rows, :]


def back_kernel(top, keys, raw, *refs):
    n = len(keys)
    parts, down_w = refs[:n], refs[n]
    held, grad_p, silu_p, act_p, dot_p = refs[n + 1 : n + 6]
    weights, (gg_ref, gu_ref, sums_ref), outs = (
        refs[n + 6 : n + 10], refs[n + 10 : n + 13], refs[n + 13 :]
    )
    back = (back_raw if raw else back_sum)(top, keys, parts, down_w, held[...])
    gg = (back * grad_p[...]).astype(BF16)
    gu = (back * silu_p[...]).astype(BF16)
    score_part = jnp.sum(back * act_p[...], axis=0, keepdims=True)
    dot_part = jnp.sum(back * dot_p[...], axis=0, keepdims=True)
    sums = jnp.concatenate(
        [score_part, dot_part, jnp.zeros((EXTRA - 2, LANES), F32)], axis=0
    )
    gg_ref[...] = gg
    gu_ref[...] = gu
    sums_ref[...] = sums
    for key, out_ref in zip(range(1, top, 2), outs):
        write_terms(top, (key,), gg, gu, sums, weights, double(out_ref))


def kept_kernel(top, keys, gg_ref, gu_ref, sums_ref, *refs):
    weights, outs = refs[:4], refs[4:]
    write_terms(top, keys, gg_ref[...], gu_ref[...], sums_ref[...], weights, outs)


def row_factors(sums, rows, wide):
    inv_rms, score = rows[0:1, :], rows[1:2, :]
    return inv_rms * inv_rms * (sums[1:2, :] / wide), sums[0:1, :] * score * (1.0 - score)


def column_kernel(top, keys, level, *refs):
    n = len(keys)
    xs, (gain_ref, router_ref, depths_ref, rows_ref), outs = refs[:n], refs[n : n + 4], refs[n + 4 :]
    active = (depths_ref[...] >= level).astype(F32)
    for n, key in enumerate(keys):
        tokens, feat = xs[n].shape
        at = overall(top, key, feat)
        outs[3 * n][...] = turned(xs[n][...]) * active
        outs[3 * n + 1][...] = column(gain_ref[:, at], tokens) * (active * rows_ref[0:1, :])
        outs[3 * n + 2][...] = column(router_ref[level - 1 : level, at], tokens) * active


def turn_kernel(first, second, first_out, second_out):
    first_out[...] = turned(first[...])
    second_out[...] = turned(second[...])


def second_kernel(wide, chip, got, cot, x, scale, router, rows_ref, out_ref):
    feat = out_ref.shape[0]
    total = chip[...] + got[...].astype(F32)
    coef, logit = row_factors(total[feat : feat + 2, :], rows_ref[...], wide)
    delta = scale[...] * total[0:feat, :] - x[...] * coef + router[...] * logit
    out_ref[...] = (cot[...].astype(F32) + delta).astype(out_ref.dtype)


def last_kernel(wide, chip, got, second, x, scale, router, rows_ref, out_ref):
    feat = out_ref.shape[1]
    total = chip[...] + got[...].astype(F32)
    coef, logit = row_factors(total[feat : feat + 2, :], rows_ref[...], wide)
    delta = scale[...] * total[0:feat, :] - x[...] * coef + router[...] * logit
    result = second[...].astype(F32) + delta
    for k in range(0, feat, LANES):
        out_ref[:, k : k + LANES] = result[k : k + LANES, :].T.astype(out_ref.dtype)


def body(hidden_first, hidden_second, cotangent, depths, norm_gain, router, w_gate, w_up, w_down):
    size = lax.axis_size("tensor")
    bits = []
    while 2 ** len(bits) < size:
        bits.append(2 ** len(bits))
    top, low = bits[-1], bits[:-1]
    tokens, feat = hidden_first.shape
    wide, units = w_gate.shape
    half = wide // 2
    product = 2 * tokens * half * units
    wide_units = VM((units, LANES), F32)
    factor_outs = [wide_units] * 4 + [VM((8, LANES), F32)]
    partial_outs = [VM((tokens, units), F32)] * 2 + [VM((2, tokens, LANES), F32)]
    grad_outs = [VM((units, LANES), BF16)] * 2 + [VM((EXTRA, LANES), F32)]
    columns = [VM((feat, tokens), F32)] * 3
    row_half = VM((half, units), BF16)
    near, across = range(top), range(top, 2 * top)
    sent, kept = range(1, top, 2), range(0, top, 2)
    block = feat + EXTRA

    def semaphores(count):
        return [pltpu.SemaphoreType.DMA((count,))]

    def reduce(grads, blocks_sent):
        parts = kernel_call(
            functools.partial(kept_kernel, top, kept),
            [VM((block, LANES), F32)] * (2 * len(kept)), *grads, *theirs, *mine,
            flops=8 * product,
        )
        blocks = dict(zip(kept, zip(parts[: len(kept)], parts[len(kept) :])))
        whole = dict(zip(sent, blocks_sent))
        for bit in low:
            for key in sorted(blocks):
                if key & bit == 0:
                    value = whole.get(key ^ bit)
                    if value is None:
                        value = jnp.concatenate(blocks[key ^ bit]).astype(BF16)
                    value = hop(value, bit).astype(F32)
                    blocks[key] = tuple(
                        own + got for own, got in zip(blocks[key], (value[:block], value[block:]))
                    )
                    blocks.pop(key ^ bit, None)
        return blocks[0]

    def back_call(keys, raw, parts, held, factors):
        *grads, = kernel_call(
            functools.partial(back_kernel, top, keys, raw),
            grad_outs + [VM((2 * block, LANES), BF16)] * len(sent),
            *parts, down, held, *factors, *theirs, *mine, flops=2 * product,
        )
        return grads[:3], grads[3:]

    x2_cross = hop(hidden_second, top)
    cot_cross = hop(cotangent, top)
    x2_mine = spread(hidden_second, low)
    cot_mine = spread(cotangent, low)
    smalls = (
        hidden_second, cotangent, hidden_first, norm_gain.reshape(1, -1), router,
        depths.reshape(1, tokens),
    )
    own_outs = partial_outs + [wide_units]
    outs = kernel_call(
        functools.partial(own_kernel, top, 1),
        [VM(a.shape, a.dtype) for a in smalls] + [row_half] * 2 + [VM(w_down.shape, BF16)] + own_outs,
        *smalls, w_gate, w_up, w_down,
        flops=3 * product // top, far=range(9),
        scratch=semaphores(6 + 2 * -(-half // PIECE) + -(-units // PIECE)),
    )
    x2_own, cot_own, x1_own, gain, router, depths, gate_mine, up_mine, down, *partial = outs
    x2_cross, *partial = lax.optimization_barrier((x2_cross, *partial))
    x2_theirs = spread(x2_cross, low)
    x1_cross = hop(after(x1_own, x2_cross), top)
    x1_mine = spread(x1_own, low)
    *partial, back_mine, gate_theirs, up_theirs = kernel_call(
        functools.partial(near_kernel, top, 1),
        own_outs + [row_half] * 2,
        *x2_mine[1:], *cot_mine[1:], gain, router, gate_mine, up_mine, down, *partial,
        w_gate, w_up, flops=3 * product * (top - 1) // top,
        far=(2 * top + 7, 2 * top + 8), scratch=semaphores(2 * -(-half // PIECE)),
    )
    mine, theirs = (gate_mine, up_mine), (gate_theirs, up_theirs)
    cot_cross, back_mine, x1_mine = lax.optimization_barrier((cot_cross, back_mine, x1_mine))
    cot_theirs = spread(cot_cross, low)
    *factors2, rows2 = kernel_call(
        functools.partial(factors_second_kernel, top, 1),
        factor_outs, *x2_theirs, gain, router, *theirs, *partial, flops=2 * product,
    )

    grads, blocks_sent = back_call(across, True, cot_theirs, back_mine, factors2)
    x1_cross, *grads = lax.optimization_barrier((x1_cross, *grads))
    x1_theirs = spread(x1_cross, low)
    chip_theirs, chip_mine = reduce(grads, blocks_sent)
    x1_theirs, chip_theirs, chip_mine = lax.optimization_barrier(
        (x1_theirs, chip_theirs, chip_mine)
    )
    got_mine = hop(chip_theirs.astype(BF16), top)
    got_theirs = hop(chip_mine.astype(BF16), top)

    rows2, chip_mine = lax.optimization_barrier((rows2, chip_mine))
    columns2 = kernel_call(
        functools.partial(column_kernel, top, (0, top), 2),
        columns * 2, x2_own, x2_cross, gain, router, depths, rows2,
    )
    cot_columns = kernel_call(turn_kernel, columns[:2], after(cot_own, rows2), cot_cross)

    x1_parts = (*x1_mine, *x1_theirs)
    *factors1, rows1 = kernel_call(
        functools.partial(factors_first_kernel, top, 0),
        factor_outs, *x1_parts, gain, router, *mine, *theirs, flops=4 * product,
    )

    def second(chip, got, cot, columns):
        return kernel_call(
            functools.partial(second_kernel, wide),
            VM((feat, tokens), BF16), chip, got, cot, *columns, rows2,
        )

    got_mine, *factors1 = lax.optimization_barrier((got_mine, *factors1))
    own_second = second(chip_mine, got_mine, cot_columns[0], columns2[:3])
    second_mine = spread(own_second, low)
    cross_second = second(chip_theirs, got_theirs, cot_columns[1], columns2[3:])
    second_theirs = spread(cross_second, low)
    back_most = kernel_call(
        functools.partial(back_part_kernel, top, (*near, top)),
        wide_units, *second_mine, cross_second, down, flops=product,
    )
    grads, blocks_sent = back_call(across[1:], False, second_theirs[1:], back_most, factors1)
    chip_theirs, chip_mine = reduce(grads, blocks_sent)
    got = hop(chip_theirs.astype(BF16), top)
    rows1 = after(rows1, chip_mine)
    columns1 = kernel_call(
        functools.partial(column_kernel, top, (0,), 1),
        columns, x1_own, gain, router, depths, rows1,
    )
    return kernel_call(
        functools.partial(last_kernel, wide),
        jax.ShapeDtypeStruct((tokens, feat), BF16),
        chip_mine, got, own_second, *columns1, rows1,
    )


def solution(mesh):
    in_specs = (
        P("dp", "tensor"),
        P("dp", "tensor"),
        P("dp", "tensor"),
        P("dp"),
        P(),
        P(),
        P(None, "tensor"),
        P(None, "tensor"),
        P("tensor", None),
    )
    out_specs = P("dp", "tensor")
    return jax.shard_map(body, mesh=mesh, in_specs=in_specs, out_specs=out_specs, check_vma=False)
```

```python
import functools

import jax
import jax.numpy as jnp
from jax import lax
from jax.experimental import pallas as pl
from jax.experimental.pallas import tpu as pltpu
from jax.sharding import PartitionSpec as P

epsilon = 1e-06
LANES = 128
EXTRA = 16
PIECE = 256
VM = pltpu.VMEM
F32 = jnp.float32
BF16 = jnp.bfloat16


def hop(value, bit):
    size = lax.axis_size("tensor")
    return lax.ppermute(value, "tensor", [(j, j ^ bit) for j in range(size)])


def after(value, *others):
    return lax.optimization_barrier((value,) + others)[0]


def spread(own, low_bits):
    parts = {0: own}
    for bit in reversed(low_bits):
        for key in list(parts):
            parts[key ^ bit] = hop(parts[key], bit)
    return [parts[key] for key in range(len(parts))]


def kernel_call(kernel, outs, *args, flops=0, far=(), scratch=()):
    many = isinstance(outs, (list, tuple))
    args = [
        pltpu.with_memory_space_constraint(a, pltpu.HBM) if n in far else a
        for n, a in enumerate(args)
    ]
    near = pl.BlockSpec(memory_space=VM)
    away = pl.BlockSpec(memory_space=pltpu.HBM)
    return pl.pallas_call(
        kernel,
        out_shape=list(outs) if many else outs,
        in_specs=[away if n in far else near for n in range(len(args))],
        out_specs=[near] * len(outs) if many else near,
        scratch_shapes=list(scratch),
        compiler_params=pltpu.CompilerParams(vmem_limit_bytes=8 * 2**20),
        cost_estimate=pl.CostEstimate(flops=6 * flops, bytes_accessed=0, transcendentals=0),
    )(*args)


def place(top):
    index = lax.axis_index("tensor")
    return index // top, index % top


def span(block, feat):
    return pl.ds(pl.multiple_of(block * feat, feat), feat)


def inside(top, key, feat):
    return span(place(top)[1] ^ (key % top), feat)


def overall(top, key, feat):
    side, inner = place(top)
    return span((side * top + inner) ^ key, feat)


def turned(value):
    value = value.astype(F32)
    return jnp.concatenate(
        [value[:, k : k + LANES].T for k in range(0, value.shape[1], LANES)], axis=0
    )


def column(row, tokens):
    return turned(jnp.broadcast_to(row, (tokens, row.shape[1])))


def mat(left, right):
    return jnp.dot(left, right, preferred_element_type=F32)


def mat_turned(left, right):
    return lax.dot_general(
        left, right, (((1,), (1,)), ((), ())), preferred_element_type=F32
    )


def fetch(sems, pairs):
    copies = []
    for n, (source, target) in enumerate(pairs):
        copy = pltpu.make_async_copy(source, target, sems.at[n])
        copy.start()
        copies.append(copy)
    return copies


def pieces(source, target):
    rows = target.shape[0]
    step = min(PIECE, rows)
    return [
        (source.at[n : n + step, :], target.at[n : n + step, :]) for n in range(0, rows, step)
    ]


def half_rows(top, far, mine):
    half = far.shape[0] // 2
    side, _ = place(top)
    return far.at[span(side if mine else 1 - side, half), :]


def norm_block(top, key, x_ref, router_row, gain_ref, router_ref, gate_w, up_w, total):
    gate, up, squares, logits = total
    feat = x_ref.shape[1]
    at, rows = overall(top, key, feat), inside(top, key, feat)
    x = x_ref[...].astype(F32)
    gained = (x * gain_ref[:, at]).astype(BF16)
    routed = x * router_ref[router_row : router_row + 1, at]
    for k in range(0, feat, LANES):
        squares = squares + x[:, k : k + LANES] * x[:, k : k + LANES]
        logits = logits + routed[:, k : k + LANES]
    gate_now, up_now = mat(gained, gate_w[rows, :]), mat(gained, up_w[rows, :])
    if gate is None:
        return gate_now, up_now, squares, logits
    return gate + gate_now, up + up_now, squares, logits


def norm_start(tokens):
    zeros = jnp.zeros((tokens, LANES), F32)
    return None, None, zeros, zeros


def own_kernel(top, router_row, *refs):
    smalls, (gate_far, up_far, down_far), small_outs, nears, outs, sems = (
        refs[:6], refs[6:9], refs[9:15], refs[15:20], refs[20:24], refs[24]
    )
    copies = fetch(
        sems,
        [
            *zip(smalls, small_outs),
            *pieces(half_rows(top, gate_far, True), nears[0]),
            *pieces(half_rows(top, up_far, True), nears[1]),
            *pieces(down_far, nears[2]),
            *pieces(half_rows(top, gate_far, False), nears[3]),
            *pieces(half_rows(top, up_far, False), nears[4]),
        ],
    )
    ready = 6 + 2 * len(pieces(nears[0], nears[0]))
    for copy in copies[:ready]:
        copy.wait()
    x, cot, _, gain_ref, router_ref, _ = small_outs
    total = norm_block(
        top, 0, x, router_row, gain_ref, router_ref, *nears[:2], norm_start(x.shape[0])
    )
    outs[0][...], outs[1][...], outs[2][0], outs[2][1] = total
    rest = ready + len(pieces(nears[2], nears[2]))
    for copy in copies[ready:rest]:
        copy.wait()
    outs[3][...] = back_raw(top, (0,), (cot,), nears[2])
    for copy in copies[rest:]:
        copy.wait()


def near_kernel(top, router_row, *refs):
    n = top - 1
    xs, cots, weights, down_w, held, outs = (
        refs[:n], refs[n : 2 * n], refs[2 * n : 2 * n + 4], refs[2 * n + 4],
        refs[2 * n + 5 : 2 * n + 9], refs[2 * n + 9 :],
    )
    total = (held[0][...], held[1][...], held[2][0], held[2][1])
    for key, x in enumerate(xs):
        total = norm_block(top, key + 1, x, router_row, *weights, total)
    outs[0][...], outs[1][...], outs[2][0], outs[2][1] = total
    outs[3][...] = back_raw(top, range(1, top), cots, down_w, held[3][...])


def write_factors(total, wide, outs):
    gate, up, squares, logits = total
    inv_rms = lax.rsqrt(jnp.sum(squares.T, axis=0, keepdims=True) / wide + epsilon)
    score = jax.nn.sigmoid(jnp.sum(logits.T, axis=0, keepdims=True))
    outs[4][...] = jnp.concatenate(
        [inv_rms, score, jnp.zeros((6, inv_rms.shape[1]), F32)], axis=0
    )
    for k in range(0, gate.shape[1], LANES):
        g = gate[:, k : k + LANES].T * inv_rms
        u = up[:, k : k + LANES].T * inv_rms
        sigma = jax.nn.sigmoid(g)
        silu = g * sigma
        grad = u * sigma * (1.0 + g * (1.0 - sigma))
        act = silu * u
        here = slice(k, k + LANES)
        outs[0][here, :] = score * grad
        outs[1][here, :] = score * silu
        outs[2][here, :] = act
        outs[3][here, :] = score * (grad * g + act)


def factors_second_kernel(top, router_row, *refs):
    xs, (gain_ref, router_ref, gate_w, up_w), held, outs = (
        refs[:top], refs[top : top + 4], refs[top + 4 : top + 7], refs[top + 7 :]
    )
    total = (held[0][...], held[1][...], held[2][0], held[2][1])
    for n, x in enumerate(xs):
        total = norm_block(top, top + n, x, router_row, gain_ref, router_ref, gate_w, up_w, total)
    write_factors(total, gain_ref.shape[1], outs)


def factors_first_kernel(top, router_row, *refs):
    xs, (gain_ref, router_ref), weights, outs = (
        refs[: 2 * top], refs[2 * top : 2 * top + 2], refs[2 * top + 2 : 2 * top + 6],
        refs[2 * top + 6 :],
    )
    total = norm_start(xs[0].shape[0])
    for key, x in enumerate(xs):
        gate_w, up_w = weights[:2] if key < top else weights[2:]
        total = norm_block(top, key, x, router_row, gain_ref, router_ref, gate_w, up_w, total)
    write_factors(total, gain_ref.shape[1], outs)


def back_raw(top, keys, parts, down_w, total=None):
    for key, part in zip(keys, parts):
        now = mat_turned(down_w[:, overall(top, key, part.shape[1])], part[...])
        total = now if total is None else total + now
    return total


def back_sum(top, keys, parts, down_w, total=None):
    for key, part in zip(keys, parts):
        now = mat(down_w[:, overall(top, key, part.shape[0])], part[...])
        total = now if total is None else total + now
    return total


def back_part_kernel(top, keys, *refs):
    n = len(keys)
    refs[n + 1][...] = back_sum(top, keys, refs[:n], refs[n])


def write_terms(top, keys, gg, gu, sums, weights, outs):
    for n, out_ref in enumerate(outs):
        gate_w, up_w = weights[2 * (n // len(keys)) : 2 * (n // len(keys)) + 2]
        feat = out_ref.shape[0] - EXTRA
        rows = inside(top, keys[n % len(keys)], feat)
        term = mat(gate_w[rows, :], gg) + mat(up_w[rows, :], gu)
        out_ref[0:feat, :] = term.astype(out_ref.dtype)
        out_ref[feat : feat + EXTRA, :] = sums.astype(out_ref.dtype)


def double(out_ref):
    rows = out_ref.shape[0] // 2
    return out_ref.at[0:rows, :], out_ref.at[rows : 2 * rows, :]


def back_kernel(top, keys, raw, *refs):
    n = len(keys)
    parts, down_w = refs[:n], refs[n]
    held, grad_p, silu_p, act_p, dot_p = refs[n + 1 : n + 6]
    weights, (gg_ref, gu_ref, sums_ref), outs = (
        refs[n + 6 : n + 10], refs[n + 10 : n + 13], refs[n + 13 :]
    )
    back = (back_raw if raw else back_sum)(top, keys, parts, down_w, held[...])
    gg = (back * grad_p[...]).astype(BF16)
    gu = (back * silu_p[...]).astype(BF16)
    score_part = jnp.sum(back * act_p[...], axis=0, keepdims=True)
    dot_part = jnp.sum(back * dot_p[...], axis=0, keepdims=True)
    sums = jnp.concatenate(
        [score_part, dot_part, jnp.zeros((EXTRA - 2, LANES), F32)], axis=0
    )
    gg_ref[...] = gg
    gu_ref[...] = gu
    sums_ref[...] = sums
    for key, out_ref in zip(range(1, top, 2), outs):
        write_terms(top, (key,), gg, gu, sums, weights, double(out_ref))


def kept_kernel(top, keys, gg_ref, gu_ref, sums_ref, *refs):
    weights, outs = refs[:4], refs[4:]
    write_terms(top, keys, gg_ref[...], gu_ref[...], sums_ref[...], weights, outs)


def row_factors(sums, rows, wide):
    inv_rms, score = rows[0:1, :], rows[1:2, :]
    return inv_rms * inv_rms * (sums[1:2, :] / wide), sums[0:1, :] * score * (1.0 - score)


def column_kernel(top, keys, level, *refs):
    n = len(keys)
    xs, (gain_ref, router_ref, depths_ref, rows_ref), outs = refs[:n], refs[n : n + 4], refs[n + 4 :]
    active = (depths_ref[...] >= level).astype(F32)
    for n, key in enumerate(keys):
        tokens, feat = xs[n].shape
        at = overall(top, key, feat)
        outs[3 * n][...] = turned(xs[n][...]) * active
        outs[3 * n + 1][...] = column(gain_ref[:, at], tokens) * (active * rows_ref[0:1, :])
        outs[3 * n + 2][...] = column(router_ref[level - 1 : level, at], tokens) * active


def turn_kernel(first, second, first_out, second_out):
    first_out[...] = turned(first[...])
    second_out[...] = turned(second[...])


def second_kernel(wide, chip, got, cot, x, scale, router, rows_ref, out_ref):
    feat = out_ref.shape[0]
    total = chip[...] + got[...].astype(F32)
    coef, logit = row_factors(total[feat : feat + 2, :], rows_ref[...], wide)
    delta = scale[...] * total[0:feat, :] - x[...] * coef + router[...] * logit
    out_ref[...] = (cot[...].astype(F32) + delta).astype(out_ref.dtype)


def last_kernel(wide, chip, got, second, x, scale, router, rows_ref, out_ref):
    feat = out_ref.shape[1]
    total = chip[...] + got[...].astype(F32)
    coef, logit = row_factors(total[feat : feat + 2, :], rows_ref[...], wide)
    delta = scale[...] * total[0:feat, :] - x[...] * coef + router[...] * logit
    result = second[...].astype(F32) + delta
    for k in range(0, feat, LANES):
        out_ref[:, k : k + LANES] = result[k : k + LANES, :].T.astype(out_ref.dtype)


def body(hidden_first, hidden_second, cotangent, depths, norm_gain, router, w_gate, w_up, w_down):
    size = lax.axis_size("tensor")
    bits = []
    while 2 ** len(bits) < size:
        bits.append(2 ** len(bits))
    top, low = bits[-1], bits[:-1]
    tokens, feat = hidden_first.shape
    wide, units = w_gate.shape
    half = wide // 2
    product = 2 * tokens * half * units
    wide_units = VM((units, LANES), F32)
    factor_outs = [wide_units] * 4 + [VM((8, LANES), F32)]
    partial_outs = [VM((tokens, units), F32)] * 2 + [VM((2, tokens, LANES), F32)]
    grad_outs = [VM((units, LANES), BF16)] * 2 + [VM((EXTRA, LANES), F32)]
    columns = [VM((feat, tokens), F32)] * 3
    row_half = VM((half, units), BF16)
    near, across = range(top), range(top, 2 * top)
    sent, kept = range(1, top, 2), range(0, top, 2)
    block = feat + EXTRA

    def semaphores(count):
        return [pltpu.SemaphoreType.DMA((count,))]

    def reduce(grads, blocks_sent):
        parts = kernel_call(
            functools.partial(kept_kernel, top, kept),
            [VM((block, LANES), F32)] * (2 * len(kept)), *grads, *theirs, *mine,
            flops=8 * product,
        )
        blocks = dict(zip(kept, zip(parts[: len(kept)], parts[len(kept) :])))
        whole = dict(zip(sent, blocks_sent))
        for bit in low:
            for key in sorted(blocks):
                if key & bit == 0:
                    value = whole.get(key ^ bit)
                    if value is None:
                        value = jnp.concatenate(blocks[key ^ bit]).astype(BF16)
                    value = hop(value, bit).astype(F32)
                    blocks[key] = tuple(
                        own + got for own, got in zip(blocks[key], (value[:block], value[block:]))
                    )
                    blocks.pop(key ^ bit, None)
        return blocks[0]

    def back_call(keys, raw, parts, held, factors):
        *grads, = kernel_call(
            functools.partial(back_kernel, top, keys, raw),
            grad_outs + [VM((2 * block, LANES), BF16)] * len(sent),
            *parts, down, held, *factors, *theirs, *mine, flops=2 * product,
        )
        return grads[:3], grads[3:]

    x2_cross = hop(hidden_second, top)
    cot_cross = hop(cotangent, top)
    x2_mine = spread(hidden_second, low)
    cot_mine = spread(cotangent, low)
    smalls = (
        hidden_second, cotangent, hidden_first, norm_gain.reshape(1, -1), router,
        depths.reshape(1, tokens),
    )
    own_outs = partial_outs + [wide_units]
    outs = kernel_call(
        functools.partial(own_kernel, top, 1),
        [VM(a.shape, a.dtype) for a in smalls]
        + [row_half] * 2 + [VM(w_down.shape, BF16)] + [row_half] * 2 + own_outs,
        *smalls, w_gate, w_up, w_down,
        flops=3 * product // top, far=range(9),
        scratch=semaphores(6 + 4 * -(-half // PIECE) + -(-units // PIECE)),
    )
    x2_own, cot_own, x1_own, gain, router, depths, gate_mine, up_mine, down = outs[:9]
    gate_theirs, up_theirs, *partial = outs[9:]
    x2_cross, *partial = lax.optimization_barrier((x2_cross, *partial))
    x2_theirs = spread(x2_cross, low)
    x1_cross = hop(hidden_first, top)
    x1_mine = spread(x1_own, low)
    *partial, back_mine = kernel_call(
        functools.partial(near_kernel, top, 1),
        own_outs,
        *x2_mine[1:], *cot_mine[1:], gain, router, gate_mine, up_mine, down, *partial,
        flops=3 * product * (top - 1) // top,
    )
    mine, theirs = (gate_mine, up_mine), (gate_theirs, up_theirs)
    cot_cross, back_mine, x1_mine = lax.optimization_barrier((cot_cross, back_mine, x1_mine))
    cot_theirs = spread(cot_cross, low)
    *factors2, rows2 = kernel_call(
        functools.partial(factors_second_kernel, top, 1),
        factor_outs, *x2_theirs, gain, router, *theirs, *partial, flops=2 * product,
    )

    grads, blocks_sent = back_call(across, True, cot_theirs, back_mine, factors2)
    x1_cross, *grads = lax.optimization_barrier((x1_cross, *grads))
    x1_theirs = spread(x1_cross, low)
    chip_theirs, chip_mine = reduce(grads, blocks_sent)
    x1_theirs, chip_theirs, chip_mine = lax.optimization_barrier(
        (x1_theirs, chip_theirs, chip_mine)
    )
    got_mine = hop(chip_theirs.astype(BF16), top)

    rows2, chip_mine = lax.optimization_barrier((rows2, chip_mine))
    columns2 = kernel_call(
        functools.partial(column_kernel, top, (0, top), 2),
        columns * 2, x2_own, x2_cross, gain, router, depths, rows2,
    )
    cot_columns = kernel_call(turn_kernel, columns[:2], after(cot_own, rows2), cot_cross)

    columns2, chip_mine = lax.optimization_barrier((columns2, chip_mine))
    got_theirs = hop(chip_mine.astype(BF16), top)
    x1_parts = (*x1_mine, *x1_theirs)
    *factors1, rows1 = kernel_call(
        functools.partial(factors_first_kernel, top, 0),
        factor_outs, *x1_parts, gain, router, *mine, *theirs, flops=4 * product,
    )

    def second(chip, got, cot, columns):
        return kernel_call(
            functools.partial(second_kernel, wide),
            VM((feat, tokens), BF16), chip, got, cot, *columns, rows2,
        )

    got_mine, *factors1 = lax.optimization_barrier((got_mine, *factors1))
    own_second = second(chip_mine, got_mine, cot_columns[0], columns2[:3])
    second_mine = spread(own_second, low)
    cross_second = second(chip_theirs, got_theirs, cot_columns[1], columns2[3:])
    second_theirs = spread(cross_second, low)
    back_most = kernel_call(
        functools.partial(back_part_kernel, top, (*near, top)),
        wide_units, *second_mine, cross_second, down, flops=product,
    )
    grads, blocks_sent = back_call(across[1:], False, second_theirs[1:], back_most, factors1)
    chip_theirs, chip_mine = reduce(grads, blocks_sent)
    got = hop(chip_theirs.astype(BF16), top)
    rows1 = after(rows1, chip_mine)
    columns1 = kernel_call(
        functools.partial(column_kernel, top, (0,), 1),
        columns, x1_own, gain, router, depths, rows1,
    )
    return kernel_call(
        functools.partial(last_kernel, wide),
        jax.ShapeDtypeStruct((tokens, feat), BF16),
        chip_mine, got, own_second, *columns1, rows1,
    )


def solution(mesh):
    in_specs = (
        P("dp", "tensor"),
        P("dp", "tensor"),
        P("dp", "tensor"),
        P("dp"),
        P(),
        P(),
        P(None, "tensor"),
        P(None, "tensor"),
        P("tensor", None),
    )
    out_specs = P("dp", "tensor")
    return jax.shard_map(body, mesh=mesh, in_specs=in_specs, out_specs=out_specs, check_vma=False)
```

```python
import functools

import jax
import jax.numpy as jnp
from jax import lax
from jax.experimental import pallas as pl
from jax.experimental.pallas import tpu as pltpu
from jax.sharding import PartitionSpec as P

epsilon = 1e-06
LANES = 128
EXTRA = 16
PIECE = 256
VM = pltpu.VMEM
F32 = jnp.float32
BF16 = jnp.bfloat16


def hop(value, bit):
    size = lax.axis_size("tensor")
    return lax.ppermute(value, "tensor", [(j, j ^ bit) for j in range(size)])


def after(value, *others):
    return lax.optimization_barrier((value,) + others)[0]


def spread(own, low_bits):
    parts = {0: own}
    for bit in reversed(low_bits):
        for key in list(parts):
            parts[key ^ bit] = hop(parts[key], bit)
    return [parts[key] for key in range(len(parts))]


def kernel_call(kernel, outs, *args, flops=0, far=(), scratch=()):
    many = isinstance(outs, (list, tuple))
    args = [
        pltpu.with_memory_space_constraint(a, pltpu.HBM) if n in far else a
        for n, a in enumerate(args)
    ]
    near = pl.BlockSpec(memory_space=VM)
    away = pl.BlockSpec(memory_space=pltpu.HBM)
    return pl.pallas_call(
        kernel,
        out_shape=list(outs) if many else outs,
        in_specs=[away if n in far else near for n in range(len(args))],
        out_specs=[near] * len(outs) if many else near,
        scratch_shapes=list(scratch),
        compiler_params=pltpu.CompilerParams(vmem_limit_bytes=8 * 2**20),
        cost_estimate=pl.CostEstimate(flops=6 * flops, bytes_accessed=0, transcendentals=0),
    )(*args)


def place(top):
    index = lax.axis_index("tensor")
    return index // top, index % top


def span(block, feat):
    return pl.ds(pl.multiple_of(block * feat, feat), feat)


def inside(top, key, feat):
    return span(place(top)[1] ^ (key % top), feat)


def overall(top, key, feat):
    side, inner = place(top)
    return span((side * top + inner) ^ key, feat)


def turned(value):
    value = value.astype(F32)
    return jnp.concatenate(
        [value[:, k : k + LANES].T for k in range(0, value.shape[1], LANES)], axis=0
    )


def column(row, tokens):
    return turned(jnp.broadcast_to(row, (tokens, row.shape[1])))


def mat(left, right):
    return jnp.dot(left, right, preferred_element_type=F32)


def mat_turned(left, right):
    return lax.dot_general(
        left, right, (((1,), (1,)), ((), ())), preferred_element_type=F32
    )


def fetch(sems, pairs):
    copies = []
    for n, (source, target) in enumerate(pairs):
        copy = pltpu.make_async_copy(source, target, sems.at[n])
        copy.start()
        copies.append(copy)
    return copies


def pieces(source, target, start, rows):
    places = [pl.ds(pl.multiple_of(start + n, PIECE), PIECE) for n in range(0, rows, PIECE)]
    return [(source.at[at, :], target.at[at, :]) for at in places]


def norm_block(top, key, x_ref, router_row, gain_ref, router_ref, gate_w, up_w, total):
    gate, up, squares, logits = total
    feat = x_ref.shape[1]
    at = overall(top, key, feat)
    x = x_ref[...].astype(F32)
    gained = (x * gain_ref[:, at]).astype(BF16)
    routed = x * router_ref[router_row : router_row + 1, at]
    for k in range(0, feat, LANES):
        squares = squares + x[:, k : k + LANES] * x[:, k : k + LANES]
        logits = logits + routed[:, k : k + LANES]
    gate_now, up_now = mat(gained, gate_w[at, :]), mat(gained, up_w[at, :])
    if gate is None:
        return gate_now, up_now, squares, logits
    return gate + gate_now, up + up_now, squares, logits


def norm_start(tokens):
    zeros = jnp.zeros((tokens, LANES), F32)
    return None, None, zeros, zeros


def own_kernel(top, router_row, *refs):
    n = top - 1
    xs, cots, refs = refs[:n], refs[n : 2 * n], refs[2 * n :]
    smalls, weights, small_outs, nears, outs, sems = (
        refs[:6], refs[6:9], refs[9:15], refs[15:18], refs[18:22], refs[22]
    )
    side, _ = place(top)
    half = weights[0].shape[0] // 2
    copies = fetch(
        sems,
        [
            *zip(smalls, small_outs),
            *pieces(weights[0], nears[0], side * half, half),
            *pieces(weights[1], nears[1], side * half, half),
            *pieces(weights[2], nears[2], 0, weights[2].shape[0]),
            *pieces(weights[0], nears[0], (1 - side) * half, half),
            *pieces(weights[1], nears[1], (1 - side) * half, half),
        ],
    )
    ready = 6 + 2 * (half // PIECE)
    rest = ready + weights[2].shape[0] // PIECE
    for copy in copies[:ready]:
        copy.wait()
    x, cot, _, gain_ref, router_ref, _ = small_outs
    total = norm_start(x.shape[0])
    for key, part in enumerate((x, *xs)):
        total = norm_block(top, key, part, router_row, gain_ref, router_ref, *nears[:2], total)
    outs[0][...], outs[1][...], outs[2][0], outs[2][1] = total
    for copy in copies[ready:rest]:
        copy.wait()
    outs[3][...] = back_raw(top, range(top), (cot, *cots), nears[2])
    for copy in copies[rest:]:
        copy.wait()


def write_factors(total, wide, outs):
    gate, up, squares, logits = total
    inv_rms = lax.rsqrt(jnp.sum(squares.T, axis=0, keepdims=True) / wide + epsilon)
    score = jax.nn.sigmoid(jnp.sum(logits.T, axis=0, keepdims=True))
    outs[4][...] = jnp.concatenate(
        [inv_rms, score, jnp.zeros((6, inv_rms.shape[1]), F32)], axis=0
    )
    for k in range(0, gate.shape[1], LANES):
        g = gate[:, k : k + LANES].T * inv_rms
        u = up[:, k : k + LANES].T * inv_rms
        sigma = jax.nn.sigmoid(g)
        silu = g * sigma
        grad = u * sigma * (1.0 + g * (1.0 - sigma))
        act = silu * u
        here = slice(k, k + LANES)
        outs[0][here, :] = score * grad
        outs[1][here, :] = score * silu
        outs[2][here, :] = act
        outs[3][here, :] = score * (grad * g + act)


def factors_second_kernel(top, router_row, *refs):
    xs, (gain_ref, router_ref, gate_w, up_w), held, outs = (
        refs[:top], refs[top : top + 4], refs[top + 4 : top + 7], refs[top + 7 :]
    )
    total = (held[0][...], held[1][...], held[2][0], held[2][1])
    for n, x in enumerate(xs):
        total = norm_block(top, top + n, x, router_row, gain_ref, router_ref, gate_w, up_w, total)
    write_factors(total, gain_ref.shape[1], outs)


def factors_first_kernel(top, router_row, *refs):
    xs, weights, outs = refs[: 2 * top], refs[2 * top : 2 * top + 4], refs[2 * top + 4 :]
    total = norm_start(xs[0].shape[0])
    for key, x in enumerate(xs):
        total = norm_block(top, key, x, router_row, *weights, total)
    write_factors(total, weights[0].shape[1], outs)


def back_raw(top, keys, parts, down_w, total=None):
    for key, part in zip(keys, parts):
        now = mat_turned(down_w[:, overall(top, key, part.shape[1])], part[...])
        total = now if total is None else total + now
    return total


def back_sum(top, keys, parts, down_w, total=None):
    for key, part in zip(keys, parts):
        now = mat(down_w[:, overall(top, key, part.shape[0])], part[...])
        total = now if total is None else total + now
    return total


def back_part_kernel(top, keys, *refs):
    n = len(keys)
    refs[n + 1][...] = back_sum(top, keys, refs[:n], refs[n])


def write_terms(top, keys, gg, gu, sums, gate_w, up_w, outs):
    for key, out_ref in zip(keys, outs):
        feat = out_ref.shape[0] - EXTRA
        rows = overall(top, key, feat)
        term = mat(gate_w[rows, :], gg) + mat(up_w[rows, :], gu)
        out_ref[0:feat, :] = term.astype(out_ref.dtype)
        out_ref[feat : feat + EXTRA, :] = sums.astype(out_ref.dtype)


def double(out_ref):
    rows = out_ref.shape[0] // 2
    return out_ref.at[0:rows, :], out_ref.at[rows : 2 * rows, :]


def back_kernel(top, keys, raw, *refs):
    n = len(keys)
    parts, down_w = refs[:n], refs[n]
    held, grad_p, silu_p, act_p, dot_p = refs[n + 1 : n + 6]
    (gate_w, up_w), (gg_ref, gu_ref, sums_ref), outs = (
        refs[n + 6 : n + 8], refs[n + 8 : n + 11], refs[n + 11 :]
    )
    back = (back_raw if raw else back_sum)(top, keys, parts, down_w, held[...])
    gg = (back * grad_p[...]).astype(BF16)
    gu = (back * silu_p[...]).astype(BF16)
    score_part = jnp.sum(back * act_p[...], axis=0, keepdims=True)
    dot_part = jnp.sum(back * dot_p[...], axis=0, keepdims=True)
    sums = jnp.concatenate(
        [score_part, dot_part, jnp.zeros((EXTRA - 2, LANES), F32)], axis=0
    )
    gg_ref[...] = gg
    gu_ref[...] = gu
    sums_ref[...] = sums
    for key, out_ref in zip(range(1, top, 2), outs):
        write_terms(top, (top + key, key), gg, gu, sums, gate_w, up_w, double(out_ref))


def kept_kernel(top, keys, gg_ref, gu_ref, sums_ref, gate_w, up_w, *outs):
    keys = [top + key for key in keys] + list(keys)
    write_terms(top, keys, gg_ref[...], gu_ref[...], sums_ref[...], gate_w, up_w, outs)


def row_factors(sums, rows, wide):
    inv_rms, score = rows[0:1, :], rows[1:2, :]
    return inv_rms * inv_rms * (sums[1:2, :] / wide), sums[0:1, :] * score * (1.0 - score)


def column_kernel(top, keys, level, *refs):
    n = len(keys)
    xs, (gain_ref, router_ref, depths_ref, rows_ref), outs = refs[:n], refs[n : n + 4], refs[n + 4 :]
    active = (depths_ref[...] >= level).astype(F32)
    for n, key in enumerate(keys):
        tokens, feat = xs[n].shape
        at = overall(top, key, feat)
        outs[3 * n][...] = turned(xs[n][...]) * active
        outs[3 * n + 1][...] = column(gain_ref[:, at], tokens) * (active * rows_ref[0:1, :])
        outs[3 * n + 2][...] = column(router_ref[level - 1 : level, at], tokens) * active


def turn_kernel(first, second, first_out, second_out):
    first_out[...] = turned(first[...])
    second_out[...] = turned(second[...])


def second_kernel(wide, chip, got, cot, x, scale, router, rows_ref, out_ref):
    feat = out_ref.shape[0]
    total = chip[...] + got[...].astype(F32)
    coef, logit = row_factors(total[feat : feat + 2, :], rows_ref[...], wide)
    delta = scale[...] * total[0:feat, :] - x[...] * coef + router[...] * logit
    out_ref[...] = (cot[...].astype(F32) + delta).astype(out_ref.dtype)


def last_kernel(wide, chip, got, second, x, scale, router, rows_ref, out_ref):
    feat = out_ref.shape[1]
    total = chip[...] + got[...].astype(F32)
    coef, logit = row_factors(total[feat : feat + 2, :], rows_ref[...], wide)
    delta = scale[...] * total[0:feat, :] - x[...] * coef + router[...] * logit
    result = second[...].astype(F32) + delta
    for k in range(0, feat, LANES):
        out_ref[:, k : k + LANES] = result[k : k + LANES, :].T.astype(out_ref.dtype)


def body(hidden_first, hidden_second, cotangent, depths, norm_gain, router, w_gate, w_up, w_down):
    size = lax.axis_size("tensor")
    bits = []
    while 2 ** len(bits) < size:
        bits.append(2 ** len(bits))
    top, low = bits[-1], bits[:-1]
    tokens, feat = hidden_first.shape
    wide, units = w_gate.shape
    half = wide // 2
    product = 2 * tokens * half * units
    wide_units = VM((units, LANES), F32)
    factor_outs = [wide_units] * 4 + [VM((8, LANES), F32)]
    partial_outs = [VM((tokens, units), F32)] * 2 + [VM((2, tokens, LANES), F32)]
    grad_outs = [VM((units, LANES), BF16)] * 2 + [VM((EXTRA, LANES), F32)]
    columns = [VM((feat, tokens), F32)] * 3
    row_half = VM((half, units), BF16)
    near, across = range(top), range(top, 2 * top)
    sent, kept = range(1, top, 2), range(0, top, 2)
    block = feat + EXTRA

    def semaphores(count):
        return [pltpu.SemaphoreType.DMA((count,))]

    def reduce(grads, blocks_sent):
        parts = kernel_call(
            functools.partial(kept_kernel, top, kept),
            [VM((block, LANES), F32)] * (2 * len(kept)), *grads, *gate_up,
            flops=8 * product,
        )
        blocks = dict(zip(kept, zip(parts[: len(kept)], parts[len(kept) :])))
        whole = dict(zip(sent, blocks_sent))
        for bit in low:
            for key in sorted(blocks):
                if key & bit == 0:
                    value = whole.get(key ^ bit)
                    if value is None:
                        value = jnp.concatenate(blocks[key ^ bit]).astype(BF16)
                    value = hop(value, bit).astype(F32)
                    blocks[key] = tuple(
                        own + got for own, got in zip(blocks[key], (value[:block], value[block:]))
                    )
                    blocks.pop(key ^ bit, None)
        return blocks[0]

    def back_call(keys, raw, parts, held, factors):
        *grads, = kernel_call(
            functools.partial(back_kernel, top, keys, raw),
            grad_outs + [VM((2 * block, LANES), BF16)] * len(sent),
            *parts, down, held, *factors, *gate_up, flops=2 * product,
        )
        return grads[:3], grads[3:]

    x2_cross = hop(hidden_second, top)
    cot_cross = hop(cotangent, top)
    x1_cross = hop(hidden_first, top)
    x2_mine = spread(hidden_second, low)
    cot_mine = spread(cotangent, low)
    smalls = (
        hidden_second, cotangent, hidden_first, norm_gain.reshape(1, -1), router,
        depths.reshape(1, tokens),
    )
    outs = kernel_call(
        functools.partial(own_kernel, top, 1),
        [VM(a.shape, a.dtype) for a in (*smalls, w_gate, w_up, w_down)]
        + partial_outs + [wide_units],
        *x2_mine[1:], *cot_mine[1:], *smalls, w_gate, w_up, w_down,
        flops=3 * product, far=range(2 * top - 2, 2 * top + 7),
        scratch=semaphores(6 + 2 * (wide // PIECE) + units // PIECE),
    )
    x2_own, cot_own, x1_own, gain, router, depths, *gate_up, down = outs[:9]
    *partial, back_mine = outs[9:]
    x2_cross, cot_cross, back_mine = lax.optimization_barrier((x2_cross, cot_cross, back_mine))
    x2_theirs = spread(x2_cross, low)
    cot_theirs = spread(cot_cross, low)
    *factors2, rows2 = kernel_call(
        functools.partial(factors_second_kernel, top, 1),
        factor_outs, *x2_theirs, gain, router, *gate_up, *partial, flops=2 * product,
    )

    grads, blocks_sent = back_call(across, True, cot_theirs, back_mine, factors2)
    x1_cross, *grads = lax.optimization_barrier((x1_cross, *grads))
    x1_mine, x1_theirs = spread(x1_own, low), spread(x1_cross, low)
    chip_theirs, chip_mine = reduce(grads, blocks_sent)
    x1_mine, x1_theirs, chip_theirs, chip_mine = lax.optimization_barrier(
        (x1_mine, x1_theirs, chip_theirs, chip_mine)
    )
    got_mine = hop(chip_theirs.astype(BF16), top)

    rows2, chip_mine = lax.optimization_barrier((rows2, chip_mine))
    columns2 = kernel_call(
        functools.partial(column_kernel, top, (0, top), 2),
        columns * 2, x2_own, x2_cross, gain, router, depths, rows2,
    )
    cot_columns = kernel_call(turn_kernel, columns[:2], after(cot_own, rows2), cot_cross)

    columns2, chip_mine = lax.optimization_barrier((columns2, chip_mine))
    got_theirs = hop(chip_mine.astype(BF16), top)
    x1_parts = (*x1_mine, *x1_theirs)
    *factors1, rows1 = kernel_call(
        functools.partial(factors_first_kernel, top, 0),
        factor_outs, *x1_parts, gain, router, *gate_up, flops=4 * product,
    )

    def second(chip, got, cot, columns):
        return kernel_call(
            functools.partial(second_kernel, wide),
            VM((feat, tokens), BF16), chip, got, cot, *columns, rows2,
        )

    got_mine, *factors1 = lax.optimization_barrier((got_mine, *factors1))
    own_second = second(chip_mine, got_mine, cot_columns[0], columns2[:3])
    second_mine = spread(own_second, low)
    cross_second = second(chip_theirs, got_theirs, cot_columns[1], columns2[3:])
    second_theirs = spread(cross_second, low)
    back_most = kernel_call(
        functools.partial(back_part_kernel, top, (*near, top)),
        wide_units, *second_mine, cross_second, down, flops=product,
    )
    grads, blocks_sent = back_call(across[1:], False, second_theirs[1:], back_most, factors1)
    chip_theirs, chip_mine = reduce(grads, blocks_sent)
    got = hop(chip_theirs.astype(BF16), top)
    rows1 = after(rows1, chip_mine)
    columns1 = kernel_call(
        functools.partial(column_kernel, top, (0,), 1),
        columns, x1_own, gain, router, depths, rows1,
    )
    return kernel_call(
        functools.partial(last_kernel, wide),
        jax.ShapeDtypeStruct((tokens, feat), BF16),
        chip_mine, got, own_second, *columns1, rows1,
    )


def solution(mesh):
    in_specs = (
        P("dp", "tensor"),
        P("dp", "tensor"),
        P("dp", "tensor"),
        P("dp"),
        P(),
        P(),
        P(None, "tensor"),
        P(None, "tensor"),
        P("tensor", None),
    )
    out_specs = P("dp", "tensor")
    return jax.shard_map(body, mesh=mesh, in_specs=in_specs, out_specs=out_specs, check_vma=False)
```

```python
import functools

import jax
import jax.numpy as jnp
from jax import lax
from jax.experimental import pallas as pl
from jax.experimental.pallas import tpu as pltpu
from jax.sharding import PartitionSpec as P

epsilon = 1e-06
LANES = 128
EXTRA = 16
PIECE = 256
VM = pltpu.VMEM
F32 = jnp.float32
BF16 = jnp.bfloat16


def hop(value, bit):
    size = lax.axis_size("tensor")
    return lax.ppermute(value, "tensor", [(j, j ^ bit) for j in range(size)])


def after(value, *others):
    return lax.optimization_barrier((value,) + others)[0]


def spread(own, low_bits):
    parts = {0: own}
    for bit in reversed(low_bits):
        for key in list(parts):
            parts[key ^ bit] = hop(parts[key], bit)
    return [parts[key] for key in range(len(parts))]


def kernel_call(kernel, outs, *args, flops=0, far=(), scratch=()):
    many = isinstance(outs, (list, tuple))
    args = [
        pltpu.with_memory_space_constraint(a, pltpu.HBM) if n in far else a
        for n, a in enumerate(args)
    ]
    near = pl.BlockSpec(memory_space=VM)
    away = pl.BlockSpec(memory_space=pltpu.HBM)
    return pl.pallas_call(
        kernel,
        out_shape=list(outs) if many else outs,
        in_specs=[away if n in far else near for n in range(len(args))],
        out_specs=[near] * len(outs) if many else near,
        scratch_shapes=list(scratch),
        compiler_params=pltpu.CompilerParams(vmem_limit_bytes=8 * 2**20),
        cost_estimate=pl.CostEstimate(flops=6 * flops, bytes_accessed=0, transcendentals=0),
    )(*args)


def place(top):
    index = lax.axis_index("tensor")
    return index // top, index % top


def span(block, feat):
    return pl.ds(pl.multiple_of(block * feat, feat), feat)


def inside(top, key, feat):
    return span(place(top)[1] ^ (key % top), feat)


def overall(top, key, feat):
    side, inner = place(top)
    return span((side * top + inner) ^ key, feat)


def turned(value):
    value = value.astype(F32)
    return jnp.concatenate(
        [value[:, k : k + LANES].T for k in range(0, value.shape[1], LANES)], axis=0
    )


def column(row, tokens):
    return turned(jnp.broadcast_to(row, (tokens, row.shape[1])))


def mat(left, right):
    return jnp.dot(left, right, preferred_element_type=F32)


def mat_turned(left, right):
    return lax.dot_general(
        left, right, (((1,), (1,)), ((), ())), preferred_element_type=F32
    )


def fetch(sems, pairs):
    copies = []
    for n, (source, target) in enumerate(pairs):
        copy = pltpu.make_async_copy(source, target, sems.at[n])
        copy.start()
        copies.append(copy)
    return copies


def pieces(source, target, start, rows):
    places = [pl.ds(pl.multiple_of(start + n, PIECE), PIECE) for n in range(0, rows, PIECE)]
    return [(source.at[at, :], target.at[at, :]) for at in places]


def norm_block(top, key, x_ref, router_row, gain_ref, router_ref, gate_w, up_w, total):
    gate, up, squares, logits = total
    feat = x_ref.shape[1]
    at = overall(top, key, feat)
    x = x_ref[...].astype(F32)
    gained = (x * gain_ref[:, at]).astype(BF16)
    routed = x * router_ref[router_row : router_row + 1, at]
    for k in range(0, feat, LANES):
        squares = squares + x[:, k : k + LANES] * x[:, k : k + LANES]
        logits = logits + routed[:, k : k + LANES]
    gate_now, up_now = mat(gained, gate_w[at, :]), mat(gained, up_w[at, :])
    if gate is None:
        return gate_now, up_now, squares, logits
    return gate + gate_now, up + up_now, squares, logits


def norm_start(tokens):
    zeros = jnp.zeros((tokens, LANES), F32)
    return None, None, zeros, zeros


def own_kernel(top, router_row, *refs):
    n = top - 1
    xs, cots, refs = refs[:n], refs[n : 2 * n], refs[2 * n :]
    smalls, weights, small_outs, nears, outs, sems = (
        refs[:6], refs[6:9], refs[9:15], refs[15:18], refs[18:22], refs[22]
    )
    side, _ = place(top)
    half = weights[0].shape[0] // 2
    copies = fetch(
        sems,
        [
            *zip(smalls, small_outs),
            *pieces(weights[0], nears[0], side * half, half),
            *pieces(weights[1], nears[1], side * half, half),
            *pieces(weights[2], nears[2], 0, weights[2].shape[0]),
            *pieces(weights[0], nears[0], (1 - side) * half, half),
            *pieces(weights[1], nears[1], (1 - side) * half, half),
        ],
    )
    ready = 6 + 2 * (half // PIECE)
    rest = ready + weights[2].shape[0] // PIECE
    for copy in copies[:ready]:
        copy.wait()
    x, cot, _, gain_ref, router_ref, _ = small_outs
    total = norm_start(x.shape[0])
    for key, part in enumerate((x, *xs)):
        total = norm_block(top, key, part, router_row, gain_ref, router_ref, *nears[:2], total)
    outs[0][...], outs[1][...], outs[2][0], outs[2][1] = total
    for copy in copies[ready:rest]:
        copy.wait()
    outs[3][...] = back_raw(top, range(top), (cot, *cots), nears[2])
    for copy in copies[rest:]:
        copy.wait()


def write_factors(total, wide, outs):
    gate, up, squares, logits = total
    inv_rms = lax.rsqrt(jnp.sum(squares.T, axis=0, keepdims=True) / wide + epsilon)
    score = jax.nn.sigmoid(jnp.sum(logits.T, axis=0, keepdims=True))
    outs[4][...] = jnp.concatenate(
        [inv_rms, score, jnp.zeros((6, inv_rms.shape[1]), F32)], axis=0
    )
    for k in range(0, gate.shape[1], LANES):
        g = gate[:, k : k + LANES].T * inv_rms
        u = up[:, k : k + LANES].T * inv_rms
        sigma = jax.nn.sigmoid(g)
        silu = g * sigma
        grad = u * sigma * (1.0 + g * (1.0 - sigma))
        act = silu * u
        here = slice(k, k + LANES)
        outs[0][here, :] = score * grad
        outs[1][here, :] = score * silu
        outs[2][here, :] = act
        outs[3][here, :] = score * (grad * g + act)


def factors_second_kernel(top, router_row, *refs):
    xs, (gain_ref, router_ref, gate_w, up_w), held, outs = (
        refs[:top], refs[top : top + 4], refs[top + 4 : top + 7], refs[top + 7 :]
    )
    total = (held[0][...], held[1][...], held[2][0], held[2][1])
    for n, x in enumerate(xs):
        total = norm_block(top, top + n, x, router_row, gain_ref, router_ref, gate_w, up_w, total)
    write_factors(total, gain_ref.shape[1], outs)


def factors_first_kernel(top, router_row, *refs):
    xs, weights, outs = refs[: 2 * top], refs[2 * top : 2 * top + 4], refs[2 * top + 4 :]
    total = norm_start(xs[0].shape[0])
    for key, x in enumerate(xs):
        total = norm_block(top, key, x, router_row, *weights, total)
    write_factors(total, weights[0].shape[1], outs)


def back_raw(top, keys, parts, down_w, total=None):
    for key, part in zip(keys, parts):
        now = mat_turned(down_w[:, overall(top, key, part.shape[1])], part[...])
        total = now if total is None else total + now
    return total


def back_sum(top, keys, parts, down_w, total=None):
    for key, part in zip(keys, parts):
        now = mat(down_w[:, overall(top, key, part.shape[0])], part[...])
        total = now if total is None else total + now
    return total


def back_part_kernel(top, keys, *refs):
    n = len(keys)
    refs[n + 1][...] = back_sum(top, keys, refs[:n], refs[n])


def write_terms(top, keys, gg, gu, sums, gate_w, up_w, outs):
    for key, out_ref in zip(keys, outs):
        feat = out_ref.shape[0] - EXTRA
        rows = overall(top, key, feat)
        term = mat(gate_w[rows, :], gg) + mat(up_w[rows, :], gu)
        out_ref[0:feat, :] = term.astype(out_ref.dtype)
        out_ref[feat : feat + EXTRA, :] = sums.astype(out_ref.dtype)


def double(out_ref):
    rows = out_ref.shape[0] // 2
    return out_ref.at[0:rows, :], out_ref.at[rows : 2 * rows, :]


def back_kernel(top, keys, raw, *refs):
    n = len(keys)
    parts, down_w = refs[:n], refs[n]
    held, grad_p, silu_p, act_p, dot_p = refs[n + 1 : n + 6]
    (gate_w, up_w), (gg_ref, gu_ref, sums_ref), outs = (
        refs[n + 6 : n + 8], refs[n + 8 : n + 11], refs[n + 11 :]
    )
    back = (back_raw if raw else back_sum)(top, keys, parts, down_w, held[...])
    gg = (back * grad_p[...]).astype(BF16)
    gu = (back * silu_p[...]).astype(BF16)
    score_part = jnp.sum(back * act_p[...], axis=0, keepdims=True)
    dot_part = jnp.sum(back * dot_p[...], axis=0, keepdims=True)
    sums = jnp.concatenate(
        [score_part, dot_part, jnp.zeros((EXTRA - 2, LANES), F32)], axis=0
    )
    gg_ref[...] = gg
    gu_ref[...] = gu
    sums_ref[...] = sums
    for key, out_ref in zip(range(1, top, 2), outs):
        write_terms(top, (top + key, key), gg, gu, sums, gate_w, up_w, double(out_ref))


def kept_kernel(top, keys, gg_ref, gu_ref, sums_ref, gate_w, up_w, *outs):
    keys = [top + key for key in keys] + list(keys)
    write_terms(top, keys, gg_ref[...], gu_ref[...], sums_ref[...], gate_w, up_w, outs)


def row_factors(sums, rows, wide):
    inv_rms, score = rows[0:1, :], rows[1:2, :]
    return inv_rms * inv_rms * (sums[1:2, :] / wide), sums[0:1, :] * score * (1.0 - score)


def column_kernel(top, keys, level, *refs):
    n = len(keys)
    xs, (gain_ref, router_ref, depths_ref, rows_ref), outs = refs[:n], refs[n : n + 4], refs[n + 4 :]
    active = (depths_ref[...] >= level).astype(F32)
    for n, key in enumerate(keys):
        tokens, feat = xs[n].shape
        at = overall(top, key, feat)
        outs[3 * n][...] = turned(xs[n][...]) * active
        outs[3 * n + 1][...] = column(gain_ref[:, at], tokens) * (active * rows_ref[0:1, :])
        outs[3 * n + 2][...] = column(router_ref[level - 1 : level, at], tokens) * active


def turn_kernel(first, second, first_out, second_out):
    first_out[...] = turned(first[...])
    second_out[...] = turned(second[...])


def second_kernel(wide, chip, got, cot, x, scale, router, rows_ref, out_ref):
    feat = out_ref.shape[0]
    total = chip[...] + got[...].astype(F32)
    coef, logit = row_factors(total[feat : feat + 2, :], rows_ref[...], wide)
    delta = scale[...] * total[0:feat, :] - x[...] * coef + router[...] * logit
    out_ref[...] = (cot[...].astype(F32) + delta).astype(out_ref.dtype)


def last_kernel(wide, chip, got, second, x, scale, router, rows_ref, out_ref):
    feat = out_ref.shape[1]
    total = chip[...] + got[...].astype(F32)
    coef, logit = row_factors(total[feat : feat + 2, :], rows_ref[...], wide)
    delta = scale[...] * total[0:feat, :] - x[...] * coef + router[...] * logit
    result = second[...].astype(F32) + delta
    for k in range(0, feat, LANES):
        out_ref[:, k : k + LANES] = result[k : k + LANES, :].T.astype(out_ref.dtype)


def body(hidden_first, hidden_second, cotangent, depths, norm_gain, router, w_gate, w_up, w_down):
    size = lax.axis_size("tensor")
    bits = []
    while 2 ** len(bits) < size:
        bits.append(2 ** len(bits))
    top, low = bits[-1], bits[:-1]
    tokens, feat = hidden_first.shape
    wide, units = w_gate.shape
    half = wide // 2
    product = 2 * tokens * half * units
    wide_units = VM((units, LANES), F32)
    factor_outs = [wide_units] * 4 + [VM((8, LANES), F32)]
    partial_outs = [VM((tokens, units), F32)] * 2 + [VM((2, tokens, LANES), F32)]
    grad_outs = [VM((units, LANES), BF16)] * 2 + [VM((EXTRA, LANES), F32)]
    columns = [VM((feat, tokens), F32)] * 3
    row_half = VM((half, units), BF16)
    near, across = range(top), range(top, 2 * top)
    sent, kept = range(1, top, 2), range(0, top, 2)
    block = feat + EXTRA

    def semaphores(count):
        return [pltpu.SemaphoreType.DMA((count,))]

    def reduce(grads, blocks_sent):
        parts = kernel_call(
            functools.partial(kept_kernel, top, kept),
            [VM((block, LANES), F32)] * (2 * len(kept)), *grads, *gate_up,
            flops=8 * product,
        )
        blocks = dict(zip(kept, zip(parts[: len(kept)], parts[len(kept) :])))
        whole = dict(zip(sent, blocks_sent))
        for bit in low:
            for key in sorted(blocks):
                if key & bit == 0:
                    value = whole.get(key ^ bit)
                    if value is None:
                        value = jnp.concatenate(blocks[key ^ bit]).astype(BF16)
                    value = hop(value, bit).astype(F32)
                    blocks[key] = tuple(
                        own + got for own, got in zip(blocks[key], (value[:block], value[block:]))
                    )
                    blocks.pop(key ^ bit, None)
        return blocks[0]

    def back_call(keys, raw, parts, held, factors):
        *grads, = kernel_call(
            functools.partial(back_kernel, top, keys, raw),
            grad_outs + [VM((2 * block, LANES), BF16)] * len(sent),
            *parts, down, held, *factors, *gate_up, flops=2 * product,
        )
        return grads[:3], grads[3:]

    x2_cross = hop(hidden_second, top)
    cot_cross = hop(cotangent, top)
    x2_mine = spread(hidden_second, low)
    cot_mine = spread(cotangent, low)
    smalls = (
        hidden_second, cotangent, hidden_first, norm_gain.reshape(1, -1), router,
        depths.reshape(1, tokens),
    )
    outs = kernel_call(
        functools.partial(own_kernel, top, 1),
        [VM(a.shape, a.dtype) for a in (*smalls, w_gate, w_up, w_down)]
        + partial_outs + [wide_units],
        *x2_mine[1:], *cot_mine[1:], *smalls, w_gate, w_up, w_down,
        flops=3 * product, far=range(2 * top - 2, 2 * top + 7),
        scratch=semaphores(6 + 2 * (wide // PIECE) + units // PIECE),
    )
    x2_own, cot_own, x1_own, gain, router, depths, *gate_up, down = outs[:9]
    *partial, back_mine = outs[9:]
    x2_cross, back_mine = lax.optimization_barrier((x2_cross, back_mine))
    x2_theirs = spread(x2_cross, low)
    x1_cross = hop(x1_own, top)
    cot_theirs = spread(after(cot_cross, back_mine), low)
    *factors2, rows2 = kernel_call(
        functools.partial(factors_second_kernel, top, 1),
        factor_outs, *x2_theirs, gain, router, *gate_up, *partial, flops=2 * product,
    )

    grads, blocks_sent = back_call(across, True, cot_theirs, back_mine, factors2)
    x1_cross, *grads = lax.optimization_barrier((x1_cross, *grads))
    x1_mine, x1_theirs = spread(x1_own, low), spread(x1_cross, low)
    chip_theirs, chip_mine = reduce(grads, blocks_sent)
    x1_mine, x1_theirs, chip_theirs, chip_mine = lax.optimization_barrier(
        (x1_mine, x1_theirs, chip_theirs, chip_mine)
    )
    got_mine = hop(chip_theirs.astype(BF16), top)

    rows2, chip_mine = lax.optimization_barrier((rows2, chip_mine))
    columns2 = kernel_call(
        functools.partial(column_kernel, top, (0, top), 2),
        columns * 2, x2_own, x2_cross, gain, router, depths, rows2,
    )
    cot_columns = kernel_call(turn_kernel, columns[:2], after(cot_own, rows2), cot_cross)

    columns2, chip_mine = lax.optimization_barrier((columns2, chip_mine))
    got_theirs = hop(chip_mine.astype(BF16), top)
    x1_parts = (*x1_mine, *x1_theirs)
    *factors1, rows1 = kernel_call(
        functools.partial(factors_first_kernel, top, 0),
        factor_outs, *x1_parts, gain, router, *gate_up, flops=4 * product,
    )

    def second(chip, got, cot, columns):
        return kernel_call(
            functools.partial(second_kernel, wide),
            VM((feat, tokens), BF16), chip, got, cot, *columns, rows2,
        )

    got_mine, *factors1 = lax.optimization_barrier((got_mine, *factors1))
    own_second = second(chip_mine, got_mine, cot_columns[0], columns2[:3])
    second_mine = spread(own_second, low)
    cross_second = second(chip_theirs, got_theirs, cot_columns[1], columns2[3:])
    second_theirs = spread(cross_second, low)
    back_most = kernel_call(
        functools.partial(back_part_kernel, top, (*near, top)),
        wide_units, *second_mine, cross_second, down, flops=product,
    )
    grads, blocks_sent = back_call(across[1:], False, second_theirs[1:], back_most, factors1)
    chip_theirs, chip_mine = reduce(grads, blocks_sent)
    got = hop(chip_theirs.astype(BF16), top)
    rows1 = after(rows1, chip_mine)
    columns1 = kernel_call(
        functools.partial(column_kernel, top, (0,), 1),
        columns, x1_own, gain, router, depths, rows1,
    )
    return kernel_call(
        functools.partial(last_kernel, wide),
        jax.ShapeDtypeStruct((tokens, feat), BF16),
        chip_mine, got, own_second, *columns1, rows1,
    )


def solution(mesh):
    in_specs = (
        P("dp", "tensor"),
        P("dp", "tensor"),
        P("dp", "tensor"),
        P("dp"),
        P(),
        P(),
        P(None, "tensor"),
        P(None, "tensor"),
        P("tensor", None),
    )
    out_specs = P("dp", "tensor")
    return jax.shard_map(body, mesh=mesh, in_specs=in_specs, out_specs=out_specs, check_vma=False)
```

```python
import functools

import jax
import jax.numpy as jnp
from jax import lax
from jax.experimental import pallas as pl
from jax.experimental.pallas import tpu as pltpu
from jax.sharding import PartitionSpec as P

epsilon = 1e-06
LANES = 128
EXTRA = 16
PIECE = 256
VM = pltpu.VMEM
F32 = jnp.float32
BF16 = jnp.bfloat16


def hop(value, bit):
    size = lax.axis_size("tensor")
    return lax.ppermute(value, "tensor", [(j, j ^ bit) for j in range(size)])


def after(value, *others):
    return lax.optimization_barrier((value,) + others)[0]


def spread(own, low_bits):
    parts = {0: own}
    for bit in reversed(low_bits):
        for key in list(parts):
            parts[key ^ bit] = hop(parts[key], bit)
    return [parts[key] for key in range(len(parts))]


def kernel_call(kernel, outs, *args, flops=0, far=(), scratch=()):
    many = isinstance(outs, (list, tuple))
    args = [
        pltpu.with_memory_space_constraint(a, pltpu.HBM) if n in far else a
        for n, a in enumerate(args)
    ]
    near = pl.BlockSpec(memory_space=VM)
    away = pl.BlockSpec(memory_space=pltpu.HBM)
    return pl.pallas_call(
        kernel,
        out_shape=list(outs) if many else outs,
        in_specs=[away if n in far else near for n in range(len(args))],
        out_specs=[near] * len(outs) if many else near,
        scratch_shapes=list(scratch),
        compiler_params=pltpu.CompilerParams(vmem_limit_bytes=8 * 2**20),
        cost_estimate=pl.CostEstimate(flops=6 * flops, bytes_accessed=0, transcendentals=0),
    )(*args)


def place(top):
    index = lax.axis_index("tensor")
    return index // top, index % top


def span(block, feat):
    return pl.ds(pl.multiple_of(block * feat, feat), feat)


def inside(top, key, feat):
    return span(place(top)[1] ^ (key % top), feat)


def overall(top, key, feat):
    side, inner = place(top)
    return span((side * top + inner) ^ key, feat)


def turned(value):
    value = value.astype(F32)
    return jnp.concatenate(
        [value[:, k : k + LANES].T for k in range(0, value.shape[1], LANES)], axis=0
    )


def column(row, tokens):
    return turned(jnp.broadcast_to(row, (tokens, row.shape[1])))


def mat(left, right):
    return jnp.dot(left, right, preferred_element_type=F32)


def mat_turned(left, right):
    return lax.dot_general(
        left, right, (((1,), (1,)), ((), ())), preferred_element_type=F32
    )


def fetch(sems, pairs):
    copies = []
    for n, (source, target) in enumerate(pairs):
        copy = pltpu.make_async_copy(source, target, sems.at[n])
        copy.start()
        copies.append(copy)
    return copies


def pieces(source, target, start, rows):
    places = [pl.ds(pl.multiple_of(start + n, PIECE), PIECE) for n in range(0, rows, PIECE)]
    return [(source.at[at, :], target.at[at, :]) for at in places]


def norm_block(top, key, x_ref, router_row, gain_ref, router_ref, gate_w, up_w, total):
    gate, up, squares, logits = total
    feat = x_ref.shape[1]
    at = overall(top, key, feat)
    x = x_ref[...].astype(F32)
    gained = (x * gain_ref[:, at]).astype(BF16)
    routed = x * router_ref[router_row : router_row + 1, at]
    for k in range(0, feat, LANES):
        squares = squares + x[:, k : k + LANES] * x[:, k : k + LANES]
        logits = logits + routed[:, k : k + LANES]
    gate_now, up_now = mat(gained, gate_w[at, :]), mat(gained, up_w[at, :])
    if gate is None:
        return gate_now, up_now, squares, logits
    return gate + gate_now, up + up_now, squares, logits


def norm_start(tokens):
    zeros = jnp.zeros((tokens, LANES), F32)
    return None, None, zeros, zeros


def own_kernel(top, router_row, *refs):
    n = top - 1
    xs, cots, refs = refs[:n], refs[n : 2 * n], refs[2 * n :]
    smalls, weights, small_outs, nears, outs, sems = (
        refs[:6], refs[6:9], refs[9:15], refs[15:18], refs[18:22], refs[22]
    )
    side, _ = place(top)
    half = weights[0].shape[0] // 2
    copies = fetch(
        sems,
        [
            *zip(smalls, small_outs),
            *pieces(weights[0], nears[0], side * half, half),
            *pieces(weights[1], nears[1], side * half, half),
            *pieces(weights[2], nears[2], 0, weights[2].shape[0]),
            *pieces(weights[0], nears[0], (1 - side) * half, half),
            *pieces(weights[1], nears[1], (1 - side) * half, half),
        ],
    )
    ready = 6 + 2 * (half // PIECE)
    rest = ready + weights[2].shape[0] // PIECE
    for copy in copies[:ready]:
        copy.wait()
    x, cot, _, gain_ref, router_ref, _ = small_outs
    total = norm_start(x.shape[0])
    for key, part in enumerate((x, *xs)):
        total = norm_block(top, key, part, router_row, gain_ref, router_ref, *nears[:2], total)
    outs[0][...], outs[1][...], outs[2][0], outs[2][1] = total
    for copy in copies[ready:rest]:
        copy.wait()
    outs[3][...] = back_raw(top, range(top), (cot, *cots), nears[2])
    for copy in copies[rest:]:
        copy.wait()


def write_factors(total, wide, outs):
    gate, up, squares, logits = total
    inv_rms = lax.rsqrt(jnp.sum(squares.T, axis=0, keepdims=True) / wide + epsilon)
    score = jax.nn.sigmoid(jnp.sum(logits.T, axis=0, keepdims=True))
    outs[4][...] = jnp.concatenate(
        [inv_rms, score, jnp.zeros((6, inv_rms.shape[1]), F32)], axis=0
    )
    for k in range(0, gate.shape[1], LANES):
        g = gate[:, k : k + LANES].T * inv_rms
        u = up[:, k : k + LANES].T * inv_rms
        sigma = jax.nn.sigmoid(g)
        silu = g * sigma
        grad = u * sigma * (1.0 + g * (1.0 - sigma))
        act = silu * u
        here = slice(k, k + LANES)
        outs[0][here, :] = score * grad
        outs[1][here, :] = score * silu
        outs[2][here, :] = act
        outs[3][here, :] = score * (grad * g + act)


def factors_second_kernel(top, router_row, *refs):
    xs, (gain_ref, router_ref, gate_w, up_w), held, outs = (
        refs[:top], refs[top : top + 4], refs[top + 4 : top + 7], refs[top + 7 :]
    )
    total = (held[0][...], held[1][...], held[2][0], held[2][1])
    for n, x in enumerate(xs):
        total = norm_block(top, top + n, x, router_row, gain_ref, router_ref, gate_w, up_w, total)
    write_factors(total, gain_ref.shape[1], outs)


def factors_first_kernel(top, router_row, *refs):
    xs, weights, outs = refs[: 2 * top], refs[2 * top : 2 * top + 4], refs[2 * top + 4 :]
    total = norm_start(xs[0].shape[0])
    for key, x in enumerate(xs):
        total = norm_block(top, key, x, router_row, *weights, total)
    write_factors(total, weights[0].shape[1], outs)


def back_raw(top, keys, parts, down_w, total=None):
    for key, part in zip(keys, parts):
        now = mat_turned(down_w[:, overall(top, key, part.shape[1])], part[...])
        total = now if total is None else total + now
    return total


def back_sum(top, keys, parts, down_w, total=None):
    for key, part in zip(keys, parts):
        now = mat(down_w[:, overall(top, key, part.shape[0])], part[...])
        total = now if total is None else total + now
    return total


def back_part_kernel(top, keys, *refs):
    n = len(keys)
    refs[n + 1][...] = back_sum(top, keys, refs[:n], refs[n])


def write_terms(top, keys, gg, gu, sums, gate_w, up_w, outs):
    for key, out_ref in zip(keys, outs):
        feat = out_ref.shape[0] - EXTRA
        rows = overall(top, key, feat)
        term = mat(gate_w[rows, :], gg) + mat(up_w[rows, :], gu)
        out_ref[0:feat, :] = term.astype(out_ref.dtype)
        out_ref[feat : feat + EXTRA, :] = sums.astype(out_ref.dtype)


def back_kernel(top, keys, raw, *refs):
    n = len(keys)
    parts, down_w = refs[:n], refs[n]
    held, grad_p, silu_p, act_p, dot_p = refs[n + 1 : n + 6]
    (gate_w, up_w), (gg_ref, gu_ref, sums_ref), outs = (
        refs[n + 6 : n + 8], refs[n + 8 : n + 11], refs[n + 11 :]
    )
    back = (back_raw if raw else back_sum)(top, keys, parts, down_w, held[...])
    gg = (back * grad_p[...]).astype(BF16)
    gu = (back * silu_p[...]).astype(BF16)
    score_part = jnp.sum(back * act_p[...], axis=0, keepdims=True)
    dot_part = jnp.sum(back * dot_p[...], axis=0, keepdims=True)
    sums = jnp.concatenate(
        [score_part, dot_part, jnp.zeros((EXTRA - 2, LANES), F32)], axis=0
    )
    gg_ref[...] = gg
    gu_ref[...] = gu
    sums_ref[...] = sums
    sent = range(1, top, 2)
    write_terms(top, (*(top + key for key in sent), *sent), gg, gu, sums, gate_w, up_w, outs)


def kept_kernel(top, keys, gg_ref, gu_ref, sums_ref, gate_w, up_w, *outs):
    write_terms(top, keys, gg_ref[...], gu_ref[...], sums_ref[...], gate_w, up_w, outs)


def row_factors(sums, rows, wide):
    inv_rms, score = rows[0:1, :], rows[1:2, :]
    return inv_rms * inv_rms * (sums[1:2, :] / wide), sums[0:1, :] * score * (1.0 - score)


def column_kernel(top, keys, level, *refs):
    n = len(keys)
    xs, (gain_ref, router_ref, depths_ref, rows_ref), outs = refs[:n], refs[n : n + 4], refs[n + 4 :]
    active = (depths_ref[...] >= level).astype(F32)
    for n, key in enumerate(keys):
        tokens, feat = xs[n].shape
        at = overall(top, key, feat)
        outs[3 * n][...] = turned(xs[n][...]) * active
        outs[3 * n + 1][...] = column(gain_ref[:, at], tokens) * (active * rows_ref[0:1, :])
        outs[3 * n + 2][...] = column(router_ref[level - 1 : level, at], tokens) * active


def turn_kernel(first, second, first_out, second_out):
    first_out[...] = turned(first[...])
    second_out[...] = turned(second[...])


def second_kernel(wide, chip, got, cot, x, scale, router, rows_ref, out_ref):
    feat = out_ref.shape[0]
    total = chip[...] + got[...].astype(F32)
    coef, logit = row_factors(total[feat : feat + 2, :], rows_ref[...], wide)
    delta = scale[...] * total[0:feat, :] - x[...] * coef + router[...] * logit
    out_ref[...] = (cot[...].astype(F32) + delta).astype(out_ref.dtype)


def last_kernel(wide, chip, got, second, x, scale, router, rows_ref, out_ref):
    feat = out_ref.shape[1]
    total = chip[...] + got[...].astype(F32)
    coef, logit = row_factors(total[feat : feat + 2, :], rows_ref[...], wide)
    delta = scale[...] * total[0:feat, :] - x[...] * coef + router[...] * logit
    result = second[...].astype(F32) + delta
    for k in range(0, feat, LANES):
        out_ref[:, k : k + LANES] = result[k : k + LANES, :].T.astype(out_ref.dtype)


def body(hidden_first, hidden_second, cotangent, depths, norm_gain, router, w_gate, w_up, w_down):
    size = lax.axis_size("tensor")
    bits = []
    while 2 ** len(bits) < size:
        bits.append(2 ** len(bits))
    top, low = bits[-1], bits[:-1]
    tokens, feat = hidden_first.shape
    wide, units = w_gate.shape
    half = wide // 2
    product = 2 * tokens * half * units
    wide_units = VM((units, LANES), F32)
    factor_outs = [wide_units] * 4 + [VM((8, LANES), F32)]
    partial_outs = [VM((tokens, units), F32)] * 2 + [VM((2, tokens, LANES), F32)]
    grad_outs = [VM((units, LANES), BF16)] * 2 + [VM((EXTRA, LANES), F32)]
    columns = [VM((feat, tokens), F32)] * 3
    row_half = VM((half, units), BF16)
    near, across = range(top), range(top, 2 * top)
    sent, kept = range(1, top, 2), range(0, top, 2)
    block = feat + EXTRA

    def semaphores(count):
        return [pltpu.SemaphoreType.DMA((count,))]

    def reduce(start, grads, blocks_sent):
        parts = kernel_call(
            functools.partial(kept_kernel, top, [start + key for key in kept]),
            [VM((block, LANES), F32)] * len(kept), *grads, *gate_up,
            flops=2 * product * len(kept) // top,
        )
        blocks = dict(zip(kept, parts)) | dict(zip(sent, blocks_sent))
        for bit in low:
            for key in sorted(blocks):
                if key & bit == 0:
                    got = hop(blocks.pop(key ^ bit).astype(BF16), bit)
                    blocks[key] = blocks[key].astype(F32) + got.astype(F32)
        return blocks[0], parts[0]

    def back_call(keys, raw, parts, held, factors):
        *grads, = kernel_call(
            functools.partial(back_kernel, top, keys, raw),
            grad_outs + [VM((block, LANES), BF16)] * (2 * len(sent)),
            *parts, down, held, *factors, *gate_up, flops=2 * product,
        )
        return grads[:3], grads[3 : 3 + len(sent)], grads[3 + len(sent) :]

    x2_cross = hop(hidden_second, top)
    cot_cross = hop(cotangent, top)
    x2_mine = spread(hidden_second, low)
    cot_mine = spread(cotangent, low)
    smalls = (
        hidden_second, cotangent, hidden_first, norm_gain.reshape(1, -1), router,
        depths.reshape(1, tokens),
    )
    outs = kernel_call(
        functools.partial(own_kernel, top, 1),
        [VM(a.shape, a.dtype) for a in (*smalls, w_gate, w_up, w_down)]
        + partial_outs + [wide_units],
        *x2_mine[1:], *cot_mine[1:], *smalls, w_gate, w_up, w_down,
        flops=3 * product, far=range(2 * top - 2, 2 * top + 7),
        scratch=semaphores(6 + 2 * (wide // PIECE) + units // PIECE),
    )
    x2_own, cot_own, x1_own, gain, router, depths, *gate_up, down = outs[:9]
    *partial, back_mine = outs[9:]
    x2_cross, back_mine = lax.optimization_barrier((x2_cross, back_mine))
    x2_theirs = spread(x2_cross, low)
    x1_cross = hop(x1_own, top)
    cot_theirs = spread(after(cot_cross, back_mine), low)
    *factors2, rows2 = kernel_call(
        functools.partial(factors_second_kernel, top, 1),
        factor_outs, *x2_theirs, gain, router, *gate_up, *partial, flops=2 * product,
    )

    grads, to_theirs, to_mine = back_call(across, True, cot_theirs, back_mine, factors2)
    chip_theirs, part = reduce(top, grads, to_theirs)
    x1_cross, part = lax.optimization_barrier((x1_cross, part))
    x1_mine, x1_theirs = spread(x1_own, low), spread(x1_cross, low)
    got_mine = hop(chip_theirs.astype(BF16), top)
    *grads, chip_theirs = lax.optimization_barrier((*grads, chip_theirs))
    chip_mine, _ = reduce(0, grads, to_mine)
    x1_mine, x1_theirs, chip_mine = lax.optimization_barrier((x1_mine, x1_theirs, chip_mine))

    rows2, chip_mine = lax.optimization_barrier((rows2, chip_mine))
    columns2 = kernel_call(
        functools.partial(column_kernel, top, (0, top), 2),
        columns * 2, x2_own, x2_cross, gain, router, depths, rows2,
    )
    cot_columns = kernel_call(turn_kernel, columns[:2], after(cot_own, rows2), cot_cross)

    got_theirs = hop(chip_mine.astype(BF16), top)
    x1_parts = (*x1_mine, *x1_theirs)
    *factors1, rows1 = kernel_call(
        functools.partial(factors_first_kernel, top, 0),
        factor_outs, *x1_parts, gain, router, *gate_up,
    )

    def second(chip, got, cot, columns):
        return kernel_call(
            functools.partial(second_kernel, wide),
            VM((feat, tokens), BF16), chip, got, cot, *columns, rows2,
        )

    got_mine, *factors1 = lax.optimization_barrier((got_mine, *factors1))
    own_second = second(chip_mine, got_mine, cot_columns[0], columns2[:3])
    second_mine = spread(own_second, low)
    cross_second = second(chip_theirs, got_theirs, cot_columns[1], columns2[3:])
    second_theirs = spread(cross_second, low)
    back_most = kernel_call(
        functools.partial(back_part_kernel, top, (*near, top)),
        wide_units, *second_mine, cross_second, down, flops=product,
    )
    grads, to_theirs, to_mine = back_call(
        across[1:], False, second_theirs[1:], back_most, factors1
    )
    chip_theirs, _ = reduce(top, grads, to_theirs)
    got = hop(chip_theirs.astype(BF16), top)
    *grads, chip_theirs = lax.optimization_barrier((*grads, chip_theirs))
    chip_mine, _ = reduce(0, grads, to_mine)
    rows1 = after(rows1, chip_mine)
    columns1 = kernel_call(
        functools.partial(column_kernel, top, (0,), 1),
        columns, x1_own, gain, router, depths, rows1,
    )
    return kernel_call(
        functools.partial(last_kernel, wide),
        jax.ShapeDtypeStruct((tokens, feat), BF16),
        chip_mine, got, own_second, *columns1, rows1,
    )


def solution(mesh):
    in_specs = (
        P("dp", "tensor"),
        P("dp", "tensor"),
        P("dp", "tensor"),
        P("dp"),
        P(),
        P(),
        P(None, "tensor"),
        P(None, "tensor"),
        P("tensor", None),
    )
    out_specs = P("dp", "tensor")
    return jax.shard_map(body, mesh=mesh, in_specs=in_specs, out_specs=out_specs, check_vma=False)
```

```python
import functools

import jax
import jax.numpy as jnp
from jax import lax
from jax.experimental import pallas as pl
from jax.experimental.pallas import tpu as pltpu
from jax.sharding import PartitionSpec as P

epsilon = 1e-06
LANES = 128
EXTRA = 16
PIECE = 256
VM = pltpu.VMEM
F32 = jnp.float32
BF16 = jnp.bfloat16


def hop(value, bit):
    size = lax.axis_size("tensor")
    return lax.ppermute(value, "tensor", [(j, j ^ bit) for j in range(size)])


def after(value, *others):
    return lax.optimization_barrier((value,) + others)[0]


def spread(own, low_bits):
    parts = {0: own}
    for bit in reversed(low_bits):
        for key in list(parts):
            parts[key ^ bit] = hop(parts[key], bit)
    return [parts[key] for key in range(len(parts))]


def kernel_call(kernel, outs, *args, flops=0, far=(), scratch=()):
    many = isinstance(outs, (list, tuple))
    args = [
        pltpu.with_memory_space_constraint(a, pltpu.HBM) if n in far else a
        for n, a in enumerate(args)
    ]
    near = pl.BlockSpec(memory_space=VM)
    away = pl.BlockSpec(memory_space=pltpu.HBM)
    return pl.pallas_call(
        kernel,
        out_shape=list(outs) if many else outs,
        in_specs=[away if n in far else near for n in range(len(args))],
        out_specs=[near] * len(outs) if many else near,
        scratch_shapes=list(scratch),
        compiler_params=pltpu.CompilerParams(vmem_limit_bytes=8 * 2**20),
        cost_estimate=pl.CostEstimate(flops=6 * flops, bytes_accessed=0, transcendentals=0),
    )(*args)


def place(top):
    index = lax.axis_index("tensor")
    return index // top, index % top


def span(block, feat):
    return pl.ds(pl.multiple_of(block * feat, feat), feat)


def inside(top, key, feat):
    return span(place(top)[1] ^ (key % top), feat)


def overall(top, key, feat):
    side, inner = place(top)
    return span((side * top + inner) ^ key, feat)


def turned(value):
    value = value.astype(F32)
    return jnp.concatenate(
        [value[:, k : k + LANES].T for k in range(0, value.shape[1], LANES)], axis=0
    )


def column(row, tokens):
    return turned(jnp.broadcast_to(row, (tokens, row.shape[1])))


def mat(left, right):
    return jnp.dot(left, right, preferred_element_type=F32)


def mat_turned(left, right):
    return lax.dot_general(
        left, right, (((1,), (1,)), ((), ())), preferred_element_type=F32
    )


def fetch(sems, pairs):
    copies = []
    for n, (source, target) in enumerate(pairs):
        copy = pltpu.make_async_copy(source, target, sems.at[n])
        copy.start()
        copies.append(copy)
    return copies


def pieces(source, target, start, rows):
    places = [pl.ds(pl.multiple_of(start + n, PIECE), PIECE) for n in range(0, rows, PIECE)]
    return [(source.at[at, :], target.at[at, :]) for at in places]


def norm_block(top, key, x_ref, router_row, gain_ref, router_ref, gate_w, up_w, total):
    gate, up, squares, logits = total
    feat = x_ref.shape[1]
    at = overall(top, key, feat)
    x = x_ref[...].astype(F32)
    gained = (x * gain_ref[:, at]).astype(BF16)
    routed = x * router_ref[router_row : router_row + 1, at]
    for k in range(0, feat, LANES):
        squares = squares + x[:, k : k + LANES] * x[:, k : k + LANES]
        logits = logits + routed[:, k : k + LANES]
    gate_now, up_now = mat(gained, gate_w[at, :]), mat(gained, up_w[at, :])
    if gate is None:
        return gate_now, up_now, squares, logits
    return gate + gate_now, up + up_now, squares, logits


def norm_start(tokens):
    zeros = jnp.zeros((tokens, LANES), F32)
    return None, None, zeros, zeros


def own_kernel(top, router_row, *refs):
    n = top - 1
    xs, cots, refs = refs[:n], refs[n : 2 * n], refs[2 * n :]
    smalls, weights, small_outs, nears, outs, sems = (
        refs[:6], refs[6:9], refs[9:15], refs[15:18], refs[18:22], refs[22]
    )
    side, _ = place(top)
    half = weights[0].shape[0] // 2
    copies = fetch(
        sems,
        [
            *zip(smalls, small_outs),
            *pieces(weights[0], nears[0], side * half, half),
            *pieces(weights[1], nears[1], side * half, half),
            *pieces(weights[2], nears[2], 0, weights[2].shape[0]),
            *pieces(weights[0], nears[0], (1 - side) * half, half),
            *pieces(weights[1], nears[1], (1 - side) * half, half),
        ],
    )
    ready = 6 + 2 * (half // PIECE)
    rest = ready + weights[2].shape[0] // PIECE
    for copy in copies[:ready]:
        copy.wait()
    x, cot, _, gain_ref, router_ref, _ = small_outs
    total = norm_start(x.shape[0])
    for key, part in enumerate((x, *xs)):
        total = norm_block(top, key, part, router_row, gain_ref, router_ref, *nears[:2], total)
    outs[0][...], outs[1][...], outs[2][0], outs[2][1] = total
    for copy in copies[ready:rest]:
        copy.wait()
    outs[3][...] = back_raw(top, range(top), (cot, *cots), nears[2])
    for copy in copies[rest:]:
        copy.wait()


def write_factors(total, wide, outs):
    gate, up, squares, logits = total
    inv_rms = lax.rsqrt(jnp.sum(squares.T, axis=0, keepdims=True) / wide + epsilon)
    score = jax.nn.sigmoid(jnp.sum(logits.T, axis=0, keepdims=True))
    outs[4][...] = jnp.concatenate(
        [inv_rms, score, jnp.zeros((6, inv_rms.shape[1]), F32)], axis=0
    )
    for k in range(0, gate.shape[1], LANES):
        g = gate[:, k : k + LANES].T * inv_rms
        u = up[:, k : k + LANES].T * inv_rms
        sigma = jax.nn.sigmoid(g)
        silu = g * sigma
        grad = u * sigma * (1.0 + g * (1.0 - sigma))
        act = silu * u
        here = slice(k, k + LANES)
        outs[0][here, :] = score * grad
        outs[1][here, :] = score * silu
        outs[2][here, :] = act
        outs[3][here, :] = score * (grad * g + act)


def factors_second_kernel(top, router_row, *refs):
    xs, (gain_ref, router_ref, gate_w, up_w), held, outs = (
        refs[:top], refs[top : top + 4], refs[top + 4 : top + 7], refs[top + 7 :]
    )
    total = (held[0][...], held[1][...], held[2][0], held[2][1])
    for n, x in enumerate(xs):
        total = norm_block(top, top + n, x, router_row, gain_ref, router_ref, gate_w, up_w, total)
    write_factors(total, gain_ref.shape[1], outs)


def factors_first_kernel(top, router_row, *refs):
    xs, weights, outs = refs[: 2 * top], refs[2 * top : 2 * top + 4], refs[2 * top + 4 :]
    total = norm_start(xs[0].shape[0])
    for key, x in enumerate(xs):
        total = norm_block(top, key, x, router_row, *weights, total)
    write_factors(total, weights[0].shape[1], outs)


def back_raw(top, keys, parts, down_w, total=None):
    for key, part in zip(keys, parts):
        now = mat_turned(down_w[:, overall(top, key, part.shape[1])], part[...])
        total = now if total is None else total + now
    return total


def back_sum(top, keys, parts, down_w, total=None):
    for key, part in zip(keys, parts):
        now = mat(down_w[:, overall(top, key, part.shape[0])], part[...])
        total = now if total is None else total + now
    return total


def back_part_kernel(top, keys, *refs):
    n = len(keys)
    refs[n + 1][...] = back_sum(top, keys, refs[:n], refs[n])


def write_terms(top, keys, gg, gu, sums, gate_w, up_w, outs):
    for key, out_ref in zip(keys, outs):
        feat = out_ref.shape[0] - EXTRA
        rows = overall(top, key, feat)
        term = mat(gate_w[rows, :], gg) + mat(up_w[rows, :], gu)
        out_ref[0:feat, :] = term.astype(out_ref.dtype)
        out_ref[feat : feat + EXTRA, :] = sums.astype(out_ref.dtype)


def back_kernel(top, keys, raw, *refs):
    n = len(keys)
    parts, down_w = refs[:n], refs[n]
    held, grad_p, silu_p, act_p, dot_p = refs[n + 1 : n + 6]
    (gate_w, up_w), (gg_ref, gu_ref, sums_ref), outs = (
        refs[n + 6 : n + 8], refs[n + 8 : n + 11], refs[n + 11 :]
    )
    back = (back_raw if raw else back_sum)(top, keys, parts, down_w, held[...])
    gg = (back * grad_p[...]).astype(BF16)
    gu = (back * silu_p[...]).astype(BF16)
    score_part = jnp.sum(back * act_p[...], axis=0, keepdims=True)
    dot_part = jnp.sum(back * dot_p[...], axis=0, keepdims=True)
    sums = jnp.concatenate(
        [score_part, dot_part, jnp.zeros((EXTRA - 2, LANES), F32)], axis=0
    )
    gg_ref[...] = gg
    gu_ref[...] = gu
    sums_ref[...] = sums
    sent = range(1, top, 2)
    write_terms(top, (*(top + key for key in sent), *sent), gg, gu, sums, gate_w, up_w, outs)


def kept_kernel(top, keys, gg_ref, gu_ref, sums_ref, gate_w, up_w, *outs):
    write_terms(top, keys, gg_ref[...], gu_ref[...], sums_ref[...], gate_w, up_w, outs)


def row_factors(sums, rows, wide):
    inv_rms, score = rows[0:1, :], rows[1:2, :]
    return inv_rms * inv_rms * (sums[1:2, :] / wide), sums[0:1, :] * score * (1.0 - score)


def column_kernel(top, keys, level, *refs):
    n = len(keys)
    xs, (gain_ref, router_ref, depths_ref, rows_ref), outs = refs[:n], refs[n : n + 4], refs[n + 4 :]
    active = (depths_ref[...] >= level).astype(F32)
    for n, key in enumerate(keys):
        tokens, feat = xs[n].shape
        at = overall(top, key, feat)
        outs[3 * n][...] = turned(xs[n][...]) * active
        outs[3 * n + 1][...] = column(gain_ref[:, at], tokens) * (active * rows_ref[0:1, :])
        outs[3 * n + 2][...] = column(router_ref[level - 1 : level, at], tokens) * active


def turn_kernel(first, second, first_out, second_out):
    first_out[...] = turned(first[...])
    second_out[...] = turned(second[...])


def second_kernel(wide, chip, got, cot, x, scale, router, rows_ref, out_ref):
    feat = out_ref.shape[0]
    total = chip[...] + got[...].astype(F32)
    coef, logit = row_factors(total[feat : feat + 2, :], rows_ref[...], wide)
    delta = scale[...] * total[0:feat, :] - x[...] * coef + router[...] * logit
    out_ref[...] = (cot[...].astype(F32) + delta).astype(out_ref.dtype)


def last_kernel(wide, chip, got, second, x, scale, router, rows_ref, out_ref):
    feat = out_ref.shape[1]
    total = chip[...] + got[...].astype(F32)
    coef, logit = row_factors(total[feat : feat + 2, :], rows_ref[...], wide)
    delta = scale[...] * total[0:feat, :] - x[...] * coef + router[...] * logit
    result = second[...].astype(F32) + delta
    for k in range(0, feat, LANES):
        out_ref[:, k : k + LANES] = result[k : k + LANES, :].T.astype(out_ref.dtype)


def body(hidden_first, hidden_second, cotangent, depths, norm_gain, router, w_gate, w_up, w_down):
    size = lax.axis_size("tensor")
    bits = []
    while 2 ** len(bits) < size:
        bits.append(2 ** len(bits))
    top, low = bits[-1], bits[:-1]
    tokens, feat = hidden_first.shape
    wide, units = w_gate.shape
    half = wide // 2
    product = 2 * tokens * half * units
    wide_units = VM((units, LANES), F32)
    factor_outs = [wide_units] * 4 + [VM((8, LANES), F32)]
    partial_outs = [VM((tokens, units), F32)] * 2 + [VM((2, tokens, LANES), F32)]
    grad_outs = [VM((units, LANES), BF16)] * 2 + [VM((EXTRA, LANES), F32)]
    columns = [VM((feat, tokens), F32)] * 3
    row_half = VM((half, units), BF16)
    near, across = range(top), range(top, 2 * top)
    sent, kept = range(1, top, 2), range(0, top, 2)
    block = feat + EXTRA

    def semaphores(count):
        return [pltpu.SemaphoreType.DMA((count,))]

    def reduce(start, grads, blocks_sent):
        parts = kernel_call(
            functools.partial(kept_kernel, top, [start + key for key in kept]),
            [VM((block, LANES), F32)] * len(kept), *grads, *gate_up,
            flops=2 * product * len(kept) // top,
        )
        blocks = dict(zip(kept, parts)) | dict(zip(sent, blocks_sent))
        for bit in low:
            for key in sorted(blocks):
                if key & bit == 0:
                    got = hop(blocks.pop(key ^ bit).astype(BF16), bit)
                    blocks[key] = blocks[key].astype(F32) + got.astype(F32)
        return blocks[0], parts[0]

    def back_call(keys, raw, parts, held, factors):
        *grads, = kernel_call(
            functools.partial(back_kernel, top, keys, raw),
            grad_outs + [VM((block, LANES), BF16)] * (2 * len(sent)),
            *parts, down, held, *factors, *gate_up, flops=2 * product,
        )
        return grads[:3], grads[3 : 3 + len(sent)], grads[3 + len(sent) :]

    x2_cross = hop(hidden_second, top)
    cot_cross = hop(cotangent, top)
    x2_mine = spread(hidden_second, low)
    cot_mine = spread(cotangent, low)
    smalls = (
        hidden_second, cotangent, hidden_first, norm_gain.reshape(1, -1), router,
        depths.reshape(1, tokens),
    )
    outs = kernel_call(
        functools.partial(own_kernel, top, 1),
        [VM(a.shape, a.dtype) for a in (*smalls, w_gate, w_up, w_down)]
        + partial_outs + [wide_units],
        *x2_mine[1:], *cot_mine[1:], *smalls, w_gate, w_up, w_down,
        flops=product // 2, far=range(2 * top - 2, 2 * top + 7),
        scratch=semaphores(6 + 2 * (wide // PIECE) + units // PIECE),
    )
    x2_own, cot_own, x1_own, gain, router, depths, *gate_up, down = outs[:9]
    *partial, back_mine = outs[9:]
    x2_cross, back_mine = lax.optimization_barrier((x2_cross, back_mine))
    x2_theirs = spread(x2_cross, low)
    x1_cross = hop(x1_own, top)
    cot_theirs = spread(after(cot_cross, back_mine), low)
    *factors2, rows2 = kernel_call(
        functools.partial(factors_second_kernel, top, 1),
        factor_outs, *x2_theirs, gain, router, *gate_up, *partial, flops=2 * product,
    )

    grads, to_theirs, to_mine = back_call(across, True, cot_theirs, back_mine, factors2)
    chip_theirs, part = reduce(top, grads, to_theirs)
    x1_cross, part = lax.optimization_barrier((x1_cross, part))
    x1_mine, x1_theirs = spread(x1_own, low), spread(x1_cross, low)
    got_mine = hop(chip_theirs.astype(BF16), top)
    *grads, chip_theirs = lax.optimization_barrier((*grads, chip_theirs))
    chip_mine, _ = reduce(0, grads, to_mine)
    x1_mine, x1_theirs, chip_mine = lax.optimization_barrier((x1_mine, x1_theirs, chip_mine))

    rows2, chip_mine = lax.optimization_barrier((rows2, chip_mine))
    columns2 = kernel_call(
        functools.partial(column_kernel, top, (0, top), 2),
        columns * 2, x2_own, x2_cross, gain, router, depths, rows2,
    )
    cot_columns = kernel_call(turn_kernel, columns[:2], after(cot_own, rows2), cot_cross)

    got_theirs = hop(chip_mine.astype(BF16), top)
    x1_parts = (*x1_mine, *x1_theirs)
    *factors1, rows1 = kernel_call(
        functools.partial(factors_first_kernel, top, 0),
        factor_outs, *x1_parts, gain, router, *gate_up,
    )

    def second(chip, got, cot, columns):
        return kernel_call(
            functools.partial(second_kernel, wide),
            VM((feat, tokens), BF16), chip, got, cot, *columns, rows2,
        )

    got_mine, *factors1 = lax.optimization_barrier((got_mine, *factors1))
    own_second = second(chip_mine, got_mine, cot_columns[0], columns2[:3])
    second_mine = spread(own_second, low)
    cross_second = second(chip_theirs, got_theirs, cot_columns[1], columns2[3:])
    second_theirs = spread(cross_second, low)
    back_most = kernel_call(
        functools.partial(back_part_kernel, top, (*near, top)),
        wide_units, *second_mine, cross_second, down, flops=product,
    )
    grads, to_theirs, to_mine = back_call(
        across[1:], False, second_theirs[1:], back_most, factors1
    )
    chip_theirs, _ = reduce(top, grads, to_theirs)
    got = hop(chip_theirs.astype(BF16), top)
    *grads, chip_theirs = lax.optimization_barrier((*grads, chip_theirs))
    chip_mine, _ = reduce(0, grads, to_mine)
    rows1 = after(rows1, chip_mine)
    columns1 = kernel_call(
        functools.partial(column_kernel, top, (0,), 1),
        columns, x1_own, gain, router, depths, rows1,
    )
    return kernel_call(
        functools.partial(last_kernel, wide),
        jax.ShapeDtypeStruct((tokens, feat), BF16),
        chip_mine, got, own_second, *columns1, rows1,
    )


def solution(mesh):
    in_specs = (
        P("dp", "tensor"),
        P("dp", "tensor"),
        P("dp", "tensor"),
        P("dp"),
        P(),
        P(),
        P(None, "tensor"),
        P(None, "tensor"),
        P("tensor", None),
    )
    out_specs = P("dp", "tensor")
    return jax.shard_map(body, mesh=mesh, in_specs=in_specs, out_specs=out_specs, check_vma=False)
```

```python
import functools

import jax
import jax.numpy as jnp
from jax import lax
from jax.experimental import pallas as pl
from jax.experimental.pallas import tpu as pltpu
from jax.sharding import PartitionSpec as P

epsilon = 1e-06
LANES = 128
EXTRA = 16
PIECE = 256
VM = pltpu.VMEM
F32 = jnp.float32
BF16 = jnp.bfloat16


def hop(value, bit):
    size = lax.axis_size("tensor")
    return lax.ppermute(value, "tensor", [(j, j ^ bit) for j in range(size)])


def after(value, *others):
    return lax.optimization_barrier((value,) + others)[0]


def spread(own, low_bits):
    parts = {0: own}
    for bit in reversed(low_bits):
        for key in list(parts):
            parts[key ^ bit] = hop(parts[key], bit)
    return [parts[key] for key in range(len(parts))]


def kernel_call(kernel, outs, *args, flops=0, far=(), scratch=(), out_far=False):
    many = isinstance(outs, (list, tuple))
    args = [
        pltpu.with_memory_space_constraint(a, pltpu.HBM) if n in far else a
        for n, a in enumerate(args)
    ]
    near = pl.BlockSpec(memory_space=VM)
    away = pl.BlockSpec(memory_space=pltpu.HBM)
    return pl.pallas_call(
        kernel,
        out_shape=list(outs) if many else outs,
        in_specs=[away if n in far else near for n in range(len(args))],
        out_specs=[near] * len(outs) if many else away if out_far else near,
        scratch_shapes=list(scratch),
        compiler_params=pltpu.CompilerParams(vmem_limit_bytes=8 * 2**20),
        cost_estimate=pl.CostEstimate(flops=6 * flops, bytes_accessed=0, transcendentals=0),
    )(*args)


def place(top):
    index = lax.axis_index("tensor")
    return index // top, index % top


def span(block, feat):
    return pl.ds(pl.multiple_of(block * feat, feat), feat)


def inside(top, key, feat):
    return span(place(top)[1] ^ (key % top), feat)


def overall(top, key, feat):
    side, inner = place(top)
    return span((side * top + inner) ^ key, feat)


def turned(value):
    value = value.astype(F32)
    return jnp.concatenate(
        [value[:, k : k + LANES].T for k in range(0, value.shape[1], LANES)], axis=0
    )


def column(row, tokens):
    return turned(jnp.broadcast_to(row, (tokens, row.shape[1])))


def mat(left, right):
    return jnp.dot(left, right, preferred_element_type=F32)


def mat_turned(left, right):
    return lax.dot_general(
        left, right, (((1,), (1,)), ((), ())), preferred_element_type=F32
    )


def fetch(sems, pairs):
    copies = []
    for n, (source, target) in enumerate(pairs):
        copy = pltpu.make_async_copy(source, target, sems.at[n])
        copy.start()
        copies.append(copy)
    return copies


def pieces(source, target, start, rows):
    places = [pl.ds(pl.multiple_of(start + n, PIECE), PIECE) for n in range(0, rows, PIECE)]
    return [(source.at[at, :], target.at[at, :]) for at in places]


def norm_block(top, key, x_ref, router_row, gain_ref, router_ref, gate_w, up_w, total):
    gate, up, squares, logits = total
    feat = x_ref.shape[1]
    at = overall(top, key, feat)
    x = x_ref[...].astype(F32)
    gained = (x * gain_ref[:, at]).astype(BF16)
    routed = x * router_ref[router_row : router_row + 1, at]
    for k in range(0, feat, LANES):
        squares = squares + x[:, k : k + LANES] * x[:, k : k + LANES]
        logits = logits + routed[:, k : k + LANES]
    gate_now, up_now = mat(gained, gate_w[at, :]), mat(gained, up_w[at, :])
    if gate is None:
        return gate_now, up_now, squares, logits
    return gate + gate_now, up + up_now, squares, logits


def norm_start(tokens):
    zeros = jnp.zeros((tokens, LANES), F32)
    return None, None, zeros, zeros


def own_kernel(top, router_row, *refs):
    n = top - 1
    xs, cots, refs = refs[:n], refs[n : 2 * n], refs[2 * n :]
    smalls, weights, small_outs, nears, outs, sems = (
        refs[:6], refs[6:9], refs[9:15], refs[15:18], refs[18:22], refs[22]
    )
    side, _ = place(top)
    half = weights[0].shape[0] // 2
    copies = fetch(
        sems,
        [
            *zip(smalls, small_outs),
            *pieces(weights[0], nears[0], side * half, half),
            *pieces(weights[1], nears[1], side * half, half),
            *pieces(weights[2], nears[2], 0, weights[2].shape[0]),
            *pieces(weights[0], nears[0], (1 - side) * half, half),
            *pieces(weights[1], nears[1], (1 - side) * half, half),
        ],
    )
    ready = 6 + 2 * (half // PIECE)
    rest = ready + weights[2].shape[0] // PIECE
    for copy in copies[:ready]:
        copy.wait()
    x, cot, _, gain_ref, router_ref, _ = small_outs
    total = norm_start(x.shape[0])
    for key, part in enumerate((x, *xs)):
        total = norm_block(top, key, part, router_row, gain_ref, router_ref, *nears[:2], total)
    outs[0][...], outs[1][...], outs[2][0], outs[2][1] = total
    for copy in copies[ready:rest]:
        copy.wait()
    outs[3][...] = back_raw(top, range(top), (cot, *cots), nears[2])
    for copy in copies[rest:]:
        copy.wait()


def write_factors(total, wide, outs):
    gate, up, squares, logits = total
    inv_rms = lax.rsqrt(jnp.sum(squares.T, axis=0, keepdims=True) / wide + epsilon)
    score = jax.nn.sigmoid(jnp.sum(logits.T, axis=0, keepdims=True))
    outs[4][...] = jnp.concatenate(
        [inv_rms, score, jnp.zeros((6, inv_rms.shape[1]), F32)], axis=0
    )
    for k in range(0, gate.shape[1], LANES):
        g = gate[:, k : k + LANES].T * inv_rms
        u = up[:, k : k + LANES].T * inv_rms
        sigma = jax.nn.sigmoid(g)
        silu = g * sigma
        grad = u * sigma * (1.0 + g * (1.0 - sigma))
        act = silu * u
        here = slice(k, k + LANES)
        outs[0][here, :] = score * grad
        outs[1][here, :] = score * silu
        outs[2][here, :] = act
        outs[3][here, :] = score * (grad * g + act)


def factors_second_kernel(top, router_row, *refs):
    xs, (gain_ref, router_ref, gate_w, up_w), held, outs = (
        refs[:top], refs[top : top + 4], refs[top + 4 : top + 7], refs[top + 7 :]
    )
    total = (held[0][...], held[1][...], held[2][0], held[2][1])
    for n, x in enumerate(xs):
        total = norm_block(top, top + n, x, router_row, gain_ref, router_ref, gate_w, up_w, total)
    write_factors(total, gain_ref.shape[1], outs)


def factors_first_kernel(top, router_row, *refs):
    xs, weights, outs = refs[: 2 * top], refs[2 * top : 2 * top + 4], refs[2 * top + 4 :]
    total = norm_start(xs[0].shape[0])
    for key, x in enumerate(xs):
        total = norm_block(top, key, x, router_row, *weights, total)
    write_factors(total, weights[0].shape[1], outs)


def back_raw(top, keys, parts, down_w, total=None):
    for key, part in zip(keys, parts):
        now = mat_turned(down_w[:, overall(top, key, part.shape[1])], part[...])
        total = now if total is None else total + now
    return total


def back_sum(top, keys, parts, down_w, total=None):
    for key, part in zip(keys, parts):
        now = mat(down_w[:, overall(top, key, part.shape[0])], part[...])
        total = now if total is None else total + now
    return total


def back_part_kernel(top, keys, *refs):
    n = len(keys)
    refs[n + 1][...] = back_sum(top, keys, refs[:n], refs[n])


def write_terms(top, keys, gg, gu, sums, gate_w, up_w, outs):
    for key, out_ref in zip(keys, outs):
        feat = out_ref.shape[0] - EXTRA
        rows = overall(top, key, feat)
        term = mat(gate_w[rows, :], gg) + mat(up_w[rows, :], gu)
        out_ref[0:feat, :] = term.astype(out_ref.dtype)
        out_ref[feat : feat + EXTRA, :] = sums.astype(out_ref.dtype)


def back_kernel(top, keys, raw, *refs):
    n = len(keys)
    parts, down_w = refs[:n], refs[n]
    held, grad_p, silu_p, act_p, dot_p = refs[n + 1 : n + 6]
    (gate_w, up_w), (gg_ref, gu_ref, sums_ref), outs = (
        refs[n + 6 : n + 8], refs[n + 8 : n + 11], refs[n + 11 :]
    )
    back = (back_raw if raw else back_sum)(top, keys, parts, down_w, held[...])
    gg = (back * grad_p[...]).astype(BF16)
    gu = (back * silu_p[...]).astype(BF16)
    score_part = jnp.sum(back * act_p[...], axis=0, keepdims=True)
    dot_part = jnp.sum(back * dot_p[...], axis=0, keepdims=True)
    sums = jnp.concatenate(
        [score_part, dot_part, jnp.zeros((EXTRA - 2, LANES), F32)], axis=0
    )
    gg_ref[...] = gg
    gu_ref[...] = gu
    sums_ref[...] = sums
    sent = range(1, top, 2)
    write_terms(top, (*(top + key for key in sent), *sent), gg, gu, sums, gate_w, up_w, outs)


def kept_kernel(top, keys, gg_ref, gu_ref, sums_ref, gate_w, up_w, *outs):
    write_terms(top, keys, gg_ref[...], gu_ref[...], sums_ref[...], gate_w, up_w, outs)


def row_factors(sums, rows, wide):
    inv_rms, score = rows[0:1, :], rows[1:2, :]
    return inv_rms * inv_rms * (sums[1:2, :] / wide), sums[0:1, :] * score * (1.0 - score)


def column_kernel(top, keys, level, *refs):
    n = len(keys)
    xs, (gain_ref, router_ref, depths_ref, rows_ref), outs = refs[:n], refs[n : n + 4], refs[n + 4 :]
    active = (depths_ref[...] >= level).astype(F32)
    for n, key in enumerate(keys):
        tokens, feat = xs[n].shape
        at = overall(top, key, feat)
        outs[3 * n][...] = turned(xs[n][...]) * active
        outs[3 * n + 1][...] = column(gain_ref[:, at], tokens) * (active * rows_ref[0:1, :])
        outs[3 * n + 2][...] = column(router_ref[level - 1 : level, at], tokens) * active


def turn_kernel(first, second, first_out, second_out):
    first_out[...] = turned(first[...])
    second_out[...] = turned(second[...])


def second_kernel(wide, chip, got, cot, x, scale, router, rows_ref, out_ref):
    feat = out_ref.shape[0]
    total = chip[...] + got[...].astype(F32)
    coef, logit = row_factors(total[feat : feat + 2, :], rows_ref[...], wide)
    delta = scale[...] * total[0:feat, :] - x[...] * coef + router[...] * logit
    out_ref[...] = (cot[...].astype(F32) + delta).astype(out_ref.dtype)


def last_kernel(wide, chip, got, second, x, scale, router, rows_ref, out_far, near, sems):
    feat = near.shape[1]
    sums = chip[feat : feat + 2, :] + got[feat : feat + 2, :].astype(F32)
    coef, logit = row_factors(sums, rows_ref[...], wide)
    copies = []
    for n, k in enumerate(range(0, feat, LANES)):
        rows = slice(k, k + LANES)
        total = chip[rows, :] + got[rows, :].astype(F32)
        delta = scale[rows, :] * total - x[rows, :] * coef + router[rows, :] * logit
        result = second[rows, :].astype(F32) + delta
        near[:, rows] = result.T.astype(near.dtype)
        copy = pltpu.make_async_copy(near.at[:, rows], out_far.at[:, rows], sems.at[n])
        copy.start()
        copies.append(copy)
    for copy in copies:
        copy.wait()


def body(hidden_first, hidden_second, cotangent, depths, norm_gain, router, w_gate, w_up, w_down):
    size = lax.axis_size("tensor")
    bits = []
    while 2 ** len(bits) < size:
        bits.append(2 ** len(bits))
    top, low = bits[-1], bits[:-1]
    tokens, feat = hidden_first.shape
    wide, units = w_gate.shape
    half = wide // 2
    product = 2 * tokens * half * units
    wide_units = VM((units, LANES), F32)
    factor_outs = [wide_units] * 4 + [VM((8, LANES), F32)]
    partial_outs = [VM((tokens, units), F32)] * 2 + [VM((2, tokens, LANES), F32)]
    grad_outs = [VM((units, LANES), BF16)] * 2 + [VM((EXTRA, LANES), F32)]
    columns = [VM((feat, tokens), F32)] * 3
    row_half = VM((half, units), BF16)
    near, across = range(top), range(top, 2 * top)
    sent, kept = range(1, top, 2), range(0, top, 2)
    block = feat + EXTRA

    def semaphores(count):
        return [pltpu.SemaphoreType.DMA((count,))]

    def reduce(start, grads, blocks_sent):
        parts = kernel_call(
            functools.partial(kept_kernel, top, [start + key for key in kept]),
            [VM((block, LANES), F32)] * len(kept), *grads, *gate_up,
            flops=2 * product * len(kept) // top,
        )
        blocks = dict(zip(kept, parts)) | dict(zip(sent, blocks_sent))
        for bit in low:
            for key in sorted(blocks):
                if key & bit == 0:
                    got = hop(blocks.pop(key ^ bit).astype(BF16), bit)
                    blocks[key] = blocks[key].astype(F32) + got.astype(F32)
        return blocks[0], parts[0]

    def back_call(keys, raw, parts, held, factors):
        *grads, = kernel_call(
            functools.partial(back_kernel, top, keys, raw),
            grad_outs + [VM((block, LANES), BF16)] * (2 * len(sent)),
            *parts, down, held, *factors, *gate_up, flops=2 * product,
        )
        return grads[:3], grads[3 : 3 + len(sent)], grads[3 + len(sent) :]

    x2_cross = hop(hidden_second, top)
    cot_cross = hop(cotangent, top)
    x2_mine = spread(hidden_second, low)
    cot_mine = spread(cotangent, low)
    smalls = (
        hidden_second, cotangent, hidden_first, norm_gain.reshape(1, -1), router,
        depths.reshape(1, tokens),
    )
    outs = kernel_call(
        functools.partial(own_kernel, top, 1),
        [VM(a.shape, a.dtype) for a in (*smalls, w_gate, w_up, w_down)]
        + partial_outs + [wide_units],
        *x2_mine[1:], *cot_mine[1:], *smalls, w_gate, w_up, w_down,
        flops=product // 2, far=range(2 * top - 2, 2 * top + 7),
        scratch=semaphores(6 + 2 * (wide // PIECE) + units // PIECE),
    )
    x2_own, cot_own, x1_own, gain, router, depths, *gate_up, down = outs[:9]
    *partial, back_mine = outs[9:]
    x2_cross, back_mine = lax.optimization_barrier((x2_cross, back_mine))
    x2_theirs = spread(x2_cross, low)
    x1_cross = hop(x1_own, top)
    cot_theirs = spread(after(cot_cross, back_mine), low)
    *factors2, rows2 = kernel_call(
        functools.partial(factors_second_kernel, top, 1),
        factor_outs, *x2_theirs, gain, router, *gate_up, *partial, flops=2 * product,
    )

    grads, to_theirs, to_mine = back_call(across, True, cot_theirs, back_mine, factors2)
    chip_theirs, part = reduce(top, grads, to_theirs)
    x1_cross, part = lax.optimization_barrier((x1_cross, part))
    x1_mine, x1_theirs = spread(x1_own, low), spread(x1_cross, low)
    got_mine = hop(chip_theirs.astype(BF16), top)
    *grads, chip_theirs = lax.optimization_barrier((*grads, chip_theirs))
    chip_mine, _ = reduce(0, grads, to_mine)

    rows2, chip_mine = lax.optimization_barrier((rows2, chip_mine))
    columns2 = kernel_call(
        functools.partial(column_kernel, top, (0, top), 2),
        columns * 2, x2_own, x2_cross, gain, router, depths, rows2,
    )
    cot_columns = kernel_call(turn_kernel, columns[:2], after(cot_own, rows2), cot_cross)

    got_theirs = hop(chip_mine.astype(BF16), top)
    x1_parts = (*x1_mine, *x1_theirs)
    *factors1, rows1 = kernel_call(
        functools.partial(factors_first_kernel, top, 0),
        factor_outs, *x1_parts, gain, router, *gate_up,
    )

    def second(chip, got, cot, columns):
        return kernel_call(
            functools.partial(second_kernel, wide),
            VM((feat, tokens), BF16), chip, got, cot, *columns, rows2,
        )

    got_mine, *factors1 = lax.optimization_barrier((got_mine, *factors1))
    own_second = second(chip_mine, got_mine, cot_columns[0], columns2[:3])
    second_mine = spread(own_second, low)
    cross_second = second(chip_theirs, got_theirs, cot_columns[1], columns2[3:])
    second_theirs = spread(cross_second, low)
    back_most = kernel_call(
        functools.partial(back_part_kernel, top, (*near, top)),
        wide_units, *second_mine, cross_second, down, flops=product,
    )
    grads, to_theirs, to_mine = back_call(
        across[1:], False, second_theirs[1:], back_most, factors1
    )
    chip_theirs, _ = reduce(top, grads, to_theirs)
    got = hop(chip_theirs.astype(BF16), top)
    *grads, chip_theirs = lax.optimization_barrier((*grads, chip_theirs))
    chip_mine, _ = reduce(0, grads, to_mine)
    rows1 = after(rows1, chip_mine)
    columns1 = kernel_call(
        functools.partial(column_kernel, top, (0,), 1),
        columns, x1_own, gain, router, depths, rows1,
    )
    return kernel_call(
        functools.partial(last_kernel, wide),
        jax.ShapeDtypeStruct((tokens, feat), BF16),
        chip_mine, got, own_second, *columns1, rows1,
        scratch=[VM((tokens, feat), BF16)] + semaphores(feat // LANES), out_far=True,
    )


def solution(mesh):
    in_specs = (
        P("dp", "tensor"),
        P("dp", "tensor"),
        P("dp", "tensor"),
        P("dp"),
        P(),
        P(),
        P(None, "tensor"),
        P(None, "tensor"),
        P("tensor", None),
    )
    out_specs = P("dp", "tensor")
    return jax.shard_map(body, mesh=mesh, in_specs=in_specs, out_specs=out_specs, check_vma=False)
```

```python
import functools

import jax
import jax.numpy as jnp
from jax import lax
from jax.experimental import pallas as pl
from jax.experimental.pallas import tpu as pltpu
from jax.sharding import PartitionSpec as P

epsilon = 1e-06
LANES = 128
EXTRA = 16
PIECE = 256
VM = pltpu.VMEM
F32 = jnp.float32
BF16 = jnp.bfloat16


def hop(value, bit):
    size = lax.axis_size("tensor")
    return lax.ppermute(value, "tensor", [(j, j ^ bit) for j in range(size)])


def after(value, *others):
    return lax.optimization_barrier((value,) + others)[0]


def spread(own, low_bits):
    parts = {0: own}
    for bit in reversed(low_bits):
        for key in list(parts):
            parts[key ^ bit] = hop(parts[key], bit)
    return [parts[key] for key in range(len(parts))]


def kernel_call(kernel, outs, *args, flops=0, far=(), scratch=(), out_far=False):
    many = isinstance(outs, (list, tuple))
    args = [
        pltpu.with_memory_space_constraint(a, pltpu.HBM) if n in far else a
        for n, a in enumerate(args)
    ]
    near = pl.BlockSpec(memory_space=VM)
    away = pl.BlockSpec(memory_space=pltpu.HBM)
    return pl.pallas_call(
        kernel,
        out_shape=list(outs) if many else outs,
        in_specs=[away if n in far else near for n in range(len(args))],
        out_specs=[near] * len(outs) if many else away if out_far else near,
        scratch_shapes=list(scratch),
        compiler_params=pltpu.CompilerParams(vmem_limit_bytes=8 * 2**20),
        cost_estimate=pl.CostEstimate(flops=6 * flops, bytes_accessed=0, transcendentals=0),
    )(*args)


def place(top):
    index = lax.axis_index("tensor")
    return index // top, index % top


def span(block, feat):
    return pl.ds(pl.multiple_of(block * feat, feat), feat)


def inside(top, key, feat):
    return span(place(top)[1] ^ (key % top), feat)


def overall(top, key, feat):
    side, inner = place(top)
    return span((side * top + inner) ^ key, feat)


def turned(value):
    value = value.astype(F32)
    return jnp.concatenate(
        [value[:, k : k + LANES].T for k in range(0, value.shape[1], LANES)], axis=0
    )


def column(row, tokens):
    return turned(jnp.broadcast_to(row, (tokens, row.shape[1])))


def mat(left, right):
    return jnp.dot(left, right, preferred_element_type=F32)


def mat_turned(left, right):
    return lax.dot_general(
        left, right, (((1,), (1,)), ((), ())), preferred_element_type=F32
    )


def fetch(sems, pairs):
    copies = []
    for n, (source, target) in enumerate(pairs):
        copy = pltpu.make_async_copy(source, target, sems.at[n])
        copy.start()
        copies.append(copy)
    return copies


def pieces(source, target, start, rows):
    places = [pl.ds(pl.multiple_of(start + n, PIECE), PIECE) for n in range(0, rows, PIECE)]
    return [(source.at[at, :], target.at[at, :]) for at in places]


def norm_block(top, key, x_ref, router_row, gain_ref, router_ref, gate_w, up_w, total):
    gate, up, squares, logits = total
    feat = x_ref.shape[1]
    at = overall(top, key, feat)
    x = x_ref[...].astype(F32)
    gained = (x * gain_ref[:, at]).astype(BF16)
    routed = x * router_ref[router_row : router_row + 1, at]
    for k in range(0, feat, LANES):
        squares = squares + x[:, k : k + LANES] * x[:, k : k + LANES]
        logits = logits + routed[:, k : k + LANES]
    gate_now, up_now = mat(gained, gate_w[at, :]), mat(gained, up_w[at, :])
    if gate is None:
        return gate_now, up_now, squares, logits
    return gate + gate_now, up + up_now, squares, logits


def norm_start(tokens):
    zeros = jnp.zeros((tokens, LANES), F32)
    return None, None, zeros, zeros


def own_kernel(top, router_row, *refs):
    n = top - 1
    xs, cots, refs = refs[:n], refs[n : 2 * n], refs[2 * n :]
    smalls, weights, small_outs, nears, outs, sems = (
        refs[:6], refs[6:9], refs[9:15], refs[15:18], refs[18:22], refs[22]
    )
    side, _ = place(top)
    half = weights[0].shape[0] // 2
    copies = fetch(
        sems,
        [
            *zip(smalls, small_outs),
            *pieces(weights[0], nears[0], side * half, half),
            *pieces(weights[1], nears[1], side * half, half),
            *pieces(weights[2], nears[2], 0, weights[2].shape[0]),
            *pieces(weights[0], nears[0], (1 - side) * half, half),
            *pieces(weights[1], nears[1], (1 - side) * half, half),
        ],
    )
    ready = 6 + 2 * (half // PIECE)
    rest = ready + weights[2].shape[0] // PIECE
    for copy in copies[:ready]:
        copy.wait()
    x, cot, _, gain_ref, router_ref, _ = small_outs
    total = norm_start(x.shape[0])
    for key, part in enumerate((x, *xs)):
        total = norm_block(top, key, part, router_row, gain_ref, router_ref, *nears[:2], total)
    outs[0][...], outs[1][...], outs[2][0], outs[2][1] = total
    for copy in copies[ready:rest]:
        copy.wait()
    outs[3][...] = back_raw(top, range(top), (cot, *cots), nears[2])
    for copy in copies[rest:]:
        copy.wait()


def write_factors(total, wide, outs):
    gate, up, squares, logits = total
    inv_rms = lax.rsqrt(jnp.sum(squares.T, axis=0, keepdims=True) / wide + epsilon)
    score = jax.nn.sigmoid(jnp.sum(logits.T, axis=0, keepdims=True))
    outs[4][...] = jnp.concatenate(
        [inv_rms, score, jnp.zeros((6, inv_rms.shape[1]), F32)], axis=0
    )
    for k in range(0, gate.shape[1], LANES):
        g = gate[:, k : k + LANES].T * inv_rms
        u = up[:, k : k + LANES].T * inv_rms
        sigma = jax.nn.sigmoid(g)
        silu = g * sigma
        grad = u * sigma * (1.0 + g * (1.0 - sigma))
        act = silu * u
        here = slice(k, k + LANES)
        outs[0][here, :] = score * grad
        outs[1][here, :] = score * silu
        outs[2][here, :] = act
        outs[3][here, :] = score * (grad * g + act)


def factors_second_kernel(top, router_row, *refs):
    xs, (gain_ref, router_ref, gate_w, up_w), held, outs = (
        refs[:top], refs[top : top + 4], refs[top + 4 : top + 7], refs[top + 7 :]
    )
    total = (held[0][...], held[1][...], held[2][0], held[2][1])
    for n, x in enumerate(xs):
        total = norm_block(top, top + n, x, router_row, gain_ref, router_ref, gate_w, up_w, total)
    write_factors(total, gain_ref.shape[1], outs)


def factors_first_kernel(top, router_row, *refs):
    xs, weights, outs = refs[: 2 * top], refs[2 * top : 2 * top + 4], refs[2 * top + 4 :]
    total = norm_start(xs[0].shape[0])
    for key, x in enumerate(xs):
        total = norm_block(top, key, x, router_row, *weights, total)
    write_factors(total, weights[0].shape[1], outs)


def back_raw(top, keys, parts, down_w, total=None):
    for key, part in zip(keys, parts):
        now = mat_turned(down_w[:, overall(top, key, part.shape[1])], part[...])
        total = now if total is None else total + now
    return total


def back_sum(top, keys, parts, down_w, total=None):
    for key, part in zip(keys, parts):
        now = mat(down_w[:, overall(top, key, part.shape[0])], part[...])
        total = now if total is None else total + now
    return total


def back_part_kernel(top, keys, *refs):
    n = len(keys)
    refs[n + 1][...] = back_sum(top, keys, refs[:n], refs[n])


def write_terms(top, keys, gg, gu, sums, gate_w, up_w, outs):
    for key, out_ref in zip(keys, outs):
        feat = out_ref.shape[0] - EXTRA
        rows = overall(top, key, feat)
        term = mat(gate_w[rows, :], gg) + mat(up_w[rows, :], gu)
        out_ref[0:feat, :] = term.astype(out_ref.dtype)
        out_ref[feat : feat + EXTRA, :] = sums.astype(out_ref.dtype)


def back_kernel(top, keys, raw, *refs):
    n = len(keys)
    parts, down_w = refs[:n], refs[n]
    held, grad_p, silu_p, act_p, dot_p = refs[n + 1 : n + 6]
    (gate_w, up_w), (gg_ref, gu_ref, sums_ref), outs = (
        refs[n + 6 : n + 8], refs[n + 8 : n + 11], refs[n + 11 :]
    )
    back = (back_raw if raw else back_sum)(top, keys, parts, down_w, held[...])
    gg = (back * grad_p[...]).astype(BF16)
    gu = (back * silu_p[...]).astype(BF16)
    score_part = jnp.sum(back * act_p[...], axis=0, keepdims=True)
    dot_part = jnp.sum(back * dot_p[...], axis=0, keepdims=True)
    sums = jnp.concatenate(
        [score_part, dot_part, jnp.zeros((EXTRA - 2, LANES), F32)], axis=0
    )
    gg_ref[...] = gg
    gu_ref[...] = gu
    sums_ref[...] = sums
    sent = range(1, top, 2)
    write_terms(top, (*(top + key for key in sent), *sent), gg, gu, sums, gate_w, up_w, outs)


def kept_kernel(top, keys, gg_ref, gu_ref, sums_ref, gate_w, up_w, *outs):
    write_terms(top, keys, gg_ref[...], gu_ref[...], sums_ref[...], gate_w, up_w, outs)


def row_factors(sums, rows, wide):
    inv_rms, score = rows[0:1, :], rows[1:2, :]
    return inv_rms * inv_rms * (sums[1:2, :] / wide), sums[0:1, :] * score * (1.0 - score)


def column_kernel(top, keys, level, *refs):
    n = len(keys)
    xs, (gain_ref, router_ref, depths_ref, rows_ref), outs = refs[:n], refs[n : n + 4], refs[n + 4 :]
    active = (depths_ref[...] >= level).astype(F32)
    for n, key in enumerate(keys):
        tokens, feat = xs[n].shape
        at = overall(top, key, feat)
        outs[3 * n][...] = turned(xs[n][...]) * active
        outs[3 * n + 1][...] = column(gain_ref[:, at], tokens) * (active * rows_ref[0:1, :])
        outs[3 * n + 2][...] = column(router_ref[level - 1 : level, at], tokens) * active


def turn_kernel(first, second, first_out, second_out):
    first_out[...] = turned(first[...])
    second_out[...] = turned(second[...])


def second_kernel(wide, chip, got, cot, x, scale, router, rows_ref, out_ref):
    feat = out_ref.shape[0]
    total = chip[...] + got[...].astype(F32)
    coef, logit = row_factors(total[feat : feat + 2, :], rows_ref[...], wide)
    delta = scale[...] * total[0:feat, :] - x[...] * coef + router[...] * logit
    out_ref[...] = (cot[...].astype(F32) + delta).astype(out_ref.dtype)


def last_kernel(wide, chip, got, second, x, scale, router, rows_ref, out_far, near, sems):
    feat = near.shape[1]
    sums = chip[feat : feat + 2, :] + got[feat : feat + 2, :].astype(F32)
    coef, logit = row_factors(sums, rows_ref[...], wide)
    copies = []
    for n, k in enumerate(range(0, feat, LANES)):
        rows = slice(k, k + LANES)
        total = chip[rows, :] + got[rows, :].astype(F32)
        delta = scale[rows, :] * total - x[rows, :] * coef + router[rows, :] * logit
        result = second[rows, :].astype(F32) + delta
        near[:, rows] = result.T.astype(near.dtype)
        copy = pltpu.make_async_copy(near.at[:, rows], out_far.at[:, rows], sems.at[n])
        copy.start()
        copies.append(copy)
    for copy in copies:
        copy.wait()


def body(hidden_first, hidden_second, cotangent, depths, norm_gain, router, w_gate, w_up, w_down):
    size = lax.axis_size("tensor")
    bits = []
    while 2 ** len(bits) < size:
        bits.append(2 ** len(bits))
    top, low = bits[-1], bits[:-1]
    tokens, feat = hidden_first.shape
    wide, units = w_gate.shape
    half = wide // 2
    product = 2 * tokens * half * units
    wide_units = VM((units, LANES), F32)
    factor_outs = [wide_units] * 4 + [VM((8, LANES), F32)]
    partial_outs = [VM((tokens, units), F32)] * 2 + [VM((2, tokens, LANES), F32)]
    grad_outs = [VM((units, LANES), BF16)] * 2 + [VM((EXTRA, LANES), F32)]
    columns = [VM((feat, tokens), F32)] * 3
    row_half = VM((half, units), BF16)
    near, across = range(top), range(top, 2 * top)
    sent, kept = range(1, top, 2), range(0, top, 2)
    block = feat + EXTRA

    def semaphores(count):
        return [pltpu.SemaphoreType.DMA((count,))]

    def reduce(start, grads, blocks_sent):
        parts = kernel_call(
            functools.partial(kept_kernel, top, [start + key for key in kept]),
            [VM((block, LANES), F32)] * len(kept), *grads, *gate_up,
            flops=2 * product * len(kept) // top,
        )
        blocks = dict(zip(kept, parts)) | dict(zip(sent, blocks_sent))
        for bit in low:
            for key in sorted(blocks):
                if key & bit == 0:
                    got = hop(blocks.pop(key ^ bit).astype(BF16), bit)
                    blocks[key] = blocks[key].astype(F32) + got.astype(F32)
        return blocks[0], parts[0]

    def back_call(keys, raw, parts, held, factors):
        *grads, = kernel_call(
            functools.partial(back_kernel, top, keys, raw),
            grad_outs + [VM((block, LANES), BF16)] * (2 * len(sent)),
            *parts, down, held, *factors, *gate_up, flops=2 * product,
        )
        return grads[:3], grads[3 : 3 + len(sent)], grads[3 + len(sent) :]

    x2_cross = hop(hidden_second, top)
    cot_cross = hop(cotangent, top)
    x2_mine = spread(hidden_second, low)
    cot_mine = spread(cotangent, low)
    smalls = (
        hidden_second, cotangent, hidden_first, norm_gain.reshape(1, -1), router,
        depths.reshape(1, tokens),
    )
    outs = kernel_call(
        functools.partial(own_kernel, top, 1),
        [VM(a.shape, a.dtype) for a in (*smalls, w_gate, w_up, w_down)]
        + partial_outs + [wide_units],
        *x2_mine[1:], *cot_mine[1:], *smalls, w_gate, w_up, w_down,
        flops=product // 2, far=range(2 * top - 2, 2 * top + 7),
        scratch=semaphores(6 + 2 * (wide // PIECE) + units // PIECE),
    )
    x2_own, cot_own, x1_own, gain, router, depths, *gate_up, down = outs[:9]
    *partial, back_mine = outs[9:]
    x2_cross, back_mine = lax.optimization_barrier((x2_cross, back_mine))
    x2_theirs = spread(x2_cross, low)
    x1_cross = hop(x1_own, top)
    cot_theirs = spread(after(cot_cross, back_mine), low)
    *factors2, rows2 = kernel_call(
        functools.partial(factors_second_kernel, top, 1),
        factor_outs, *x2_theirs, gain, router, *gate_up, *partial, flops=2 * product,
    )

    grads, to_theirs, to_mine = back_call(across, True, cot_theirs, back_mine, factors2)
    chip_theirs, part = reduce(top, grads, to_theirs)
    x1_cross, part = lax.optimization_barrier((x1_cross, part))
    x1_mine = spread(x1_own, low)
    got_mine = hop(chip_theirs.astype(BF16), top)
    *grads, chip_theirs = lax.optimization_barrier((*grads, chip_theirs))
    chip_mine, part = reduce(0, grads, to_mine)
    x1_theirs = spread(after(x1_cross, part), low)

    rows2, chip_mine = lax.optimization_barrier((rows2, chip_mine))
    columns2 = kernel_call(
        functools.partial(column_kernel, top, (0, top), 2),
        columns * 2, x2_own, x2_cross, gain, router, depths, rows2,
    )
    cot_columns = kernel_call(turn_kernel, columns[:2], after(cot_own, rows2), cot_cross)

    got_theirs = hop(chip_mine.astype(BF16), top)
    x1_parts = (*x1_mine, *x1_theirs)
    *factors1, rows1 = kernel_call(
        functools.partial(factors_first_kernel, top, 0),
        factor_outs, *x1_parts, gain, router, *gate_up,
    )

    def second(chip, got, cot, columns):
        return kernel_call(
            functools.partial(second_kernel, wide),
            VM((feat, tokens), BF16), chip, got, cot, *columns, rows2,
        )

    got_mine, *factors1 = lax.optimization_barrier((got_mine, *factors1))
    own_second = second(chip_mine, got_mine, cot_columns[0], columns2[:3])
    second_mine = spread(own_second, low)
    cross_second = second(chip_theirs, got_theirs, cot_columns[1], columns2[3:])
    second_theirs = spread(cross_second, low)
    back_most = kernel_call(
        functools.partial(back_part_kernel, top, (*near, top)),
        wide_units, *second_mine, cross_second, down, flops=product,
    )
    grads, to_theirs, to_mine = back_call(
        across[1:], False, second_theirs[1:], back_most, factors1
    )
    chip_theirs, _ = reduce(top, grads, to_theirs)
    got = hop(chip_theirs.astype(BF16), top)
    *grads, chip_theirs = lax.optimization_barrier((*grads, chip_theirs))
    chip_mine, _ = reduce(0, grads, to_mine)
    rows1 = after(rows1, chip_mine)
    columns1 = kernel_call(
        functools.partial(column_kernel, top, (0,), 1),
        columns, x1_own, gain, router, depths, rows1,
    )
    return kernel_call(
        functools.partial(last_kernel, wide),
        jax.ShapeDtypeStruct((tokens, feat), BF16),
        chip_mine, got, own_second, *columns1, rows1,
        scratch=[VM((tokens, feat), BF16)] + semaphores(feat // LANES), out_far=True,
    )


def solution(mesh):
    in_specs = (
        P("dp", "tensor"),
        P("dp", "tensor"),
        P("dp", "tensor"),
        P("dp"),
        P(),
        P(),
        P(None, "tensor"),
        P(None, "tensor"),
        P("tensor", None),
    )
    out_specs = P("dp", "tensor")
    return jax.shard_map(body, mesh=mesh, in_specs=in_specs, out_specs=out_specs, check_vma=False)
```

```python
import functools

import jax
import jax.numpy as jnp
from jax import lax
from jax.experimental import pallas as pl
from jax.experimental.pallas import tpu as pltpu
from jax.sharding import PartitionSpec as P

epsilon = 1e-06
LANES = 128
EXTRA = 16
PIECE = 512
VM = pltpu.VMEM
F32 = jnp.float32
BF16 = jnp.bfloat16


def hop(value, bit):
    size = lax.axis_size("tensor")
    return lax.ppermute(value, "tensor", [(j, j ^ bit) for j in range(size)])


def after(value, *others):
    return lax.optimization_barrier((value,) + others)[0]


def spread(own, low_bits):
    parts = {0: own}
    for bit in reversed(low_bits):
        for key in list(parts):
            parts[key ^ bit] = hop(parts[key], bit)
    return [parts[key] for key in range(len(parts))]


def kernel_call(kernel, outs, *args, flops=0, far=(), scratch=(), out_far=False):
    many = isinstance(outs, (list, tuple))
    args = [
        pltpu.with_memory_space_constraint(a, pltpu.HBM) if n in far else a
        for n, a in enumerate(args)
    ]
    near = pl.BlockSpec(memory_space=VM)
    away = pl.BlockSpec(memory_space=pltpu.HBM)
    return pl.pallas_call(
        kernel,
        out_shape=list(outs) if many else outs,
        in_specs=[away if n in far else near for n in range(len(args))],
        out_specs=[near] * len(outs) if many else away if out_far else near,
        scratch_shapes=list(scratch),
        compiler_params=pltpu.CompilerParams(vmem_limit_bytes=8 * 2**20),
        cost_estimate=pl.CostEstimate(flops=6 * flops, bytes_accessed=0, transcendentals=0),
    )(*args)


def place(top):
    index = lax.axis_index("tensor")
    return index // top, index % top


def span(block, feat):
    return pl.ds(pl.multiple_of(block * feat, feat), feat)


def inside(top, key, feat):
    return span(place(top)[1] ^ (key % top), feat)


def overall(top, key, feat):
    side, inner = place(top)
    return span((side * top + inner) ^ key, feat)


def turned(value):
    value = value.astype(F32)
    return jnp.concatenate(
        [value[:, k : k + LANES].T for k in range(0, value.shape[1], LANES)], axis=0
    )


def column(row, tokens):
    return turned(jnp.broadcast_to(row, (tokens, row.shape[1])))


def mat(left, right):
    return jnp.dot(left, right, preferred_element_type=F32)


def mat_turned(left, right):
    return lax.dot_general(
        left, right, (((1,), (1,)), ((), ())), preferred_element_type=F32
    )


def fetch(sems, pairs):
    copies = []
    for n, (source, target) in enumerate(pairs):
        copy = pltpu.make_async_copy(source, target, sems.at[n])
        copy.start()
        copies.append(copy)
    return copies


def pieces(source, target, start, rows):
    places = [pl.ds(pl.multiple_of(start + n, PIECE), PIECE) for n in range(0, rows, PIECE)]
    return [(source.at[at, :], target.at[at, :]) for at in places]


def norm_block(top, key, x_ref, router_row, gain_ref, router_ref, gate_w, up_w, total):
    gate, up, squares, logits = total
    feat = x_ref.shape[1]
    at = overall(top, key, feat)
    x = x_ref[...].astype(F32)
    gained = (x * gain_ref[:, at]).astype(BF16)
    routed = x * router_ref[router_row : router_row + 1, at]
    for k in range(0, feat, LANES):
        squares = squares + x[:, k : k + LANES] * x[:, k : k + LANES]
        logits = logits + routed[:, k : k + LANES]
    gate_now, up_now = mat(gained, gate_w[at, :]), mat(gained, up_w[at, :])
    if gate is None:
        return gate_now, up_now, squares, logits
    return gate + gate_now, up + up_now, squares, logits


def norm_start(tokens):
    zeros = jnp.zeros((tokens, LANES), F32)
    return None, None, zeros, zeros


def own_kernel(top, router_row, *refs):
    n = top - 1
    xs, cots, refs = refs[:n], refs[n : 2 * n], refs[2 * n :]
    smalls, weights, small_outs, nears, outs, sems = (
        refs[:6], refs[6:9], refs[9:15], refs[15:18], refs[18:22], refs[22]
    )
    side, _ = place(top)
    half = weights[0].shape[0] // 2
    copies = fetch(
        sems,
        [
            *zip(smalls, small_outs),
            *pieces(weights[0], nears[0], side * half, half),
            *pieces(weights[1], nears[1], side * half, half),
            *pieces(weights[2], nears[2], 0, weights[2].shape[0]),
            *pieces(weights[0], nears[0], (1 - side) * half, half),
            *pieces(weights[1], nears[1], (1 - side) * half, half),
        ],
    )
    ready = 6 + 2 * (half // PIECE)
    rest = ready + weights[2].shape[0] // PIECE
    for copy in copies[:ready]:
        copy.wait()
    x, cot, _, gain_ref, router_ref, _ = small_outs
    total = norm_start(x.shape[0])
    for key, part in enumerate((x, *xs)):
        total = norm_block(top, key, part, router_row, gain_ref, router_ref, *nears[:2], total)
    outs[0][...], outs[1][...], outs[2][0], outs[2][1] = total
    for copy in copies[ready:rest]:
        copy.wait()
    outs[3][...] = back_raw(top, range(top), (cot, *cots), nears[2])
    for copy in copies[rest:]:
        copy.wait()


def write_factors(total, wide, outs):
    gate, up, squares, logits = total
    inv_rms = lax.rsqrt(jnp.sum(squares.T, axis=0, keepdims=True) / wide + epsilon)
    score = jax.nn.sigmoid(jnp.sum(logits.T, axis=0, keepdims=True))
    outs[4][...] = jnp.concatenate(
        [inv_rms, score, jnp.zeros((6, inv_rms.shape[1]), F32)], axis=0
    )
    for k in range(0, gate.shape[1], LANES):
        g = gate[:, k : k + LANES].T * inv_rms
        u = up[:, k : k + LANES].T * inv_rms
        sigma = jax.nn.sigmoid(g)
        silu = g * sigma
        grad = u * sigma * (1.0 + g * (1.0 - sigma))
        act = silu * u
        here = slice(k, k + LANES)
        outs[0][here, :] = score * grad
        outs[1][here, :] = score * silu
        outs[2][here, :] = act
        outs[3][here, :] = score * (grad * g + act)


def factors_second_kernel(top, router_row, *refs):
    xs, (gain_ref, router_ref, gate_w, up_w), held, outs = (
        refs[:top], refs[top : top + 4], refs[top + 4 : top + 7], refs[top + 7 :]
    )
    total = (held[0][...], held[1][...], held[2][0], held[2][1])
    for n, x in enumerate(xs):
        total = norm_block(top, top + n, x, router_row, gain_ref, router_ref, gate_w, up_w, total)
    write_factors(total, gain_ref.shape[1], outs)


def factors_first_kernel(top, router_row, *refs):
    xs, weights, outs = refs[: 2 * top], refs[2 * top : 2 * top + 4], refs[2 * top + 4 :]
    total = norm_start(xs[0].shape[0])
    for key, x in enumerate(xs):
        total = norm_block(top, key, x, router_row, *weights, total)
    write_factors(total, weights[0].shape[1], outs)


def back_raw(top, keys, parts, down_w, total=None):
    for key, part in zip(keys, parts):
        now = mat_turned(down_w[:, overall(top, key, part.shape[1])], part[...])
        total = now if total is None else total + now
    return total


def back_sum(top, keys, parts, down_w, total=None):
    for key, part in zip(keys, parts):
        now = mat(down_w[:, overall(top, key, part.shape[0])], part[...])
        total = now if total is None else total + now
    return total


def back_part_kernel(top, keys, *refs):
    n = len(keys)
    refs[n + 1][...] = back_sum(top, keys, refs[:n], refs[n])


def write_terms(top, keys, gg, gu, sums, gate_w, up_w, outs):
    for key, out_ref in zip(keys, outs):
        feat = out_ref.shape[0] - EXTRA
        rows = overall(top, key, feat)
        term = mat(gate_w[rows, :], gg) + mat(up_w[rows, :], gu)
        out_ref[0:feat, :] = term.astype(out_ref.dtype)
        out_ref[feat : feat + EXTRA, :] = sums.astype(out_ref.dtype)


def back_kernel(top, keys, raw, *refs):
    n = len(keys)
    parts, down_w = refs[:n], refs[n]
    held, grad_p, silu_p, act_p, dot_p = refs[n + 1 : n + 6]
    (gate_w, up_w), (gg_ref, gu_ref, sums_ref), outs = (
        refs[n + 6 : n + 8], refs[n + 8 : n + 11], refs[n + 11 :]
    )
    back = (back_raw if raw else back_sum)(top, keys, parts, down_w, held[...])
    gg = (back * grad_p[...]).astype(BF16)
    gu = (back * silu_p[...]).astype(BF16)
    score_part = jnp.sum(back * act_p[...], axis=0, keepdims=True)
    dot_part = jnp.sum(back * dot_p[...], axis=0, keepdims=True)
    sums = jnp.concatenate(
        [score_part, dot_part, jnp.zeros((EXTRA - 2, LANES), F32)], axis=0
    )
    gg_ref[...] = gg
    gu_ref[...] = gu
    sums_ref[...] = sums
    sent = range(1, top, 2)
    write_terms(top, (*(top + key for key in sent), *sent), gg, gu, sums, gate_w, up_w, outs)


def kept_kernel(top, keys, gg_ref, gu_ref, sums_ref, gate_w, up_w, *outs):
    write_terms(top, keys, gg_ref[...], gu_ref[...], sums_ref[...], gate_w, up_w, outs)


def row_factors(sums, rows, wide):
    inv_rms, score = rows[0:1, :], rows[1:2, :]
    return inv_rms * inv_rms * (sums[1:2, :] / wide), sums[0:1, :] * score * (1.0 - score)


def column_kernel(top, keys, level, *refs):
    n = len(keys)
    xs, (gain_ref, router_ref, depths_ref, rows_ref), outs = refs[:n], refs[n : n + 4], refs[n + 4 :]
    active = (depths_ref[...] >= level).astype(F32)
    for n, key in enumerate(keys):
        tokens, feat = xs[n].shape
        at = overall(top, key, feat)
        outs[3 * n][...] = turned(xs[n][...]) * active
        outs[3 * n + 1][...] = column(gain_ref[:, at], tokens) * (active * rows_ref[0:1, :])
        outs[3 * n + 2][...] = column(router_ref[level - 1 : level, at], tokens) * active


def turn_kernel(first, second, first_out, second_out):
    first_out[...] = turned(first[...])
    second_out[...] = turned(second[...])


def second_kernel(wide, chip, got, cot, x, scale, router, rows_ref, out_ref):
    feat = out_ref.shape[0]
    total = chip[...] + got[...].astype(F32)
    coef, logit = row_factors(total[feat : feat + 2, :], rows_ref[...], wide)
    delta = scale[...] * total[0:feat, :] - x[...] * coef + router[...] * logit
    out_ref[...] = (cot[...].astype(F32) + delta).astype(out_ref.dtype)


def last_kernel(wide, chip, got, second, x, scale, router, rows_ref, out_far, near, sems):
    feat = near.shape[1]
    sums = chip[feat : feat + 2, :] + got[feat : feat + 2, :].astype(F32)
    coef, logit = row_factors(sums, rows_ref[...], wide)
    copies = []
    for n, k in enumerate(range(0, feat, LANES)):
        rows = slice(k, k + LANES)
        total = chip[rows, :] + got[rows, :].astype(F32)
        delta = scale[rows, :] * total - x[rows, :] * coef + router[rows, :] * logit
        result = second[rows, :].astype(F32) + delta
        near[:, rows] = result.T.astype(near.dtype)
        copy = pltpu.make_async_copy(near.at[:, rows], out_far.at[:, rows], sems.at[n])
        copy.start()
        copies.append(copy)
    for copy in copies:
        copy.wait()


def body(hidden_first, hidden_second, cotangent, depths, norm_gain, router, w_gate, w_up, w_down):
    size = lax.axis_size("tensor")
    bits = []
    while 2 ** len(bits) < size:
        bits.append(2 ** len(bits))
    top, low = bits[-1], bits[:-1]
    tokens, feat = hidden_first.shape
    wide, units = w_gate.shape
    half = wide // 2
    product = 2 * tokens * half * units
    wide_units = VM((units, LANES), F32)
    factor_outs = [wide_units] * 4 + [VM((8, LANES), F32)]
    partial_outs = [VM((tokens, units), F32)] * 2 + [VM((2, tokens, LANES), F32)]
    grad_outs = [VM((units, LANES), BF16)] * 2 + [VM((EXTRA, LANES), F32)]
    columns = [VM((feat, tokens), F32)] * 3
    row_half = VM((half, units), BF16)
    near, across = range(top), range(top, 2 * top)
    sent, kept = range(1, top, 2), range(0, top, 2)
    block = feat + EXTRA

    def semaphores(count):
        return [pltpu.SemaphoreType.DMA((count,))]

    def reduce(start, grads, blocks_sent):
        parts = kernel_call(
            functools.partial(kept_kernel, top, [start + key for key in kept]),
            [VM((block, LANES), F32)] * len(kept), *grads, *gate_up,
            flops=2 * product * len(kept) // top,
        )
        blocks = dict(zip(kept, parts)) | dict(zip(sent, blocks_sent))
        for bit in low:
            for key in sorted(blocks):
                if key & bit == 0:
                    got = hop(blocks.pop(key ^ bit).astype(BF16), bit)
                    blocks[key] = blocks[key].astype(F32) + got.astype(F32)
        return blocks[0], parts[0]

    def back_call(keys, raw, parts, held, factors):
        *grads, = kernel_call(
            functools.partial(back_kernel, top, keys, raw),
            grad_outs + [VM((block, LANES), BF16)] * (2 * len(sent)),
            *parts, down, held, *factors, *gate_up, flops=2 * product,
        )
        return grads[:3], grads[3 : 3 + len(sent)], grads[3 + len(sent) :]

    x2_cross = hop(hidden_second, top)
    cot_cross = hop(cotangent, top)
    x2_mine = spread(hidden_second, low)
    cot_mine = spread(cotangent, low)
    smalls = (
        hidden_second, cotangent, hidden_first, norm_gain.reshape(1, -1), router,
        depths.reshape(1, tokens),
    )
    outs = kernel_call(
        functools.partial(own_kernel, top, 1),
        [VM(a.shape, a.dtype) for a in (*smalls, w_gate, w_up, w_down)]
        + partial_outs + [wide_units],
        *x2_mine[1:], *cot_mine[1:], *smalls, w_gate, w_up, w_down,
        flops=product // 2, far=range(2 * top - 2, 2 * top + 7),
        scratch=semaphores(6 + 2 * (wide // PIECE) + units // PIECE),
    )
    x2_own, cot_own, x1_own, gain, router, depths, *gate_up, down = outs[:9]
    *partial, back_mine = outs[9:]
    x2_cross, back_mine = lax.optimization_barrier((x2_cross, back_mine))
    x2_theirs = spread(x2_cross, low)
    x1_cross = hop(x1_own, top)
    cot_theirs = spread(after(cot_cross, back_mine), low)
    *factors2, rows2 = kernel_call(
        functools.partial(factors_second_kernel, top, 1),
        factor_outs, *x2_theirs, gain, router, *gate_up, *partial, flops=2 * product,
    )

    grads, to_theirs, to_mine = back_call(across, True, cot_theirs, back_mine, factors2)
    chip_theirs, part = reduce(top, grads, to_theirs)
    x1_cross, part = lax.optimization_barrier((x1_cross, part))
    x1_mine = spread(x1_own, low)
    got_mine = hop(chip_theirs.astype(BF16), top)
    *grads, chip_theirs = lax.optimization_barrier((*grads, chip_theirs))
    chip_mine, part = reduce(0, grads, to_mine)
    x1_theirs = spread(after(x1_cross, part), low)

    rows2, chip_mine = lax.optimization_barrier((rows2, chip_mine))
    columns2 = kernel_call(
        functools.partial(column_kernel, top, (0, top), 2),
        columns * 2, x2_own, x2_cross, gain, router, depths, rows2,
    )
    cot_columns = kernel_call(turn_kernel, columns[:2], after(cot_own, rows2), cot_cross)

    got_theirs = hop(chip_mine.astype(BF16), top)
    x1_parts = (*x1_mine, *x1_theirs)
    *factors1, rows1 = kernel_call(
        functools.partial(factors_first_kernel, top, 0),
        factor_outs, *x1_parts, gain, router, *gate_up,
    )

    def second(chip, got, cot, columns):
        return kernel_call(
            functools.partial(second_kernel, wide),
            VM((feat, tokens), BF16), chip, got, cot, *columns, rows2,
        )

    got_mine, *factors1 = lax.optimization_barrier((got_mine, *factors1))
    own_second = second(chip_mine, got_mine, cot_columns[0], columns2[:3])
    second_mine = spread(own_second, low)
    cross_second = second(chip_theirs, got_theirs, cot_columns[1], columns2[3:])
    second_theirs = spread(cross_second, low)
    back_most = kernel_call(
        functools.partial(back_part_kernel, top, (*near, top)),
        wide_units, *second_mine, cross_second, down, flops=product,
    )
    grads, to_theirs, to_mine = back_call(
        across[1:], False, second_theirs[1:], back_most, factors1
    )
    chip_theirs, _ = reduce(top, grads, to_theirs)
    got = hop(chip_theirs.astype(BF16), top)
    *grads, chip_theirs = lax.optimization_barrier((*grads, chip_theirs))
    chip_mine, _ = reduce(0, grads, to_mine)
    rows1 = after(rows1, chip_mine)
    columns1 = kernel_call(
        functools.partial(column_kernel, top, (0,), 1),
        columns, x1_own, gain, router, depths, rows1,
    )
    return kernel_call(
        functools.partial(last_kernel, wide),
        jax.ShapeDtypeStruct((tokens, feat), BF16),
        chip_mine, got, own_second, *columns1, rows1,
        scratch=[VM((tokens, feat), BF16)] + semaphores(feat // LANES), out_far=True,
    )


def solution(mesh):
    in_specs = (
        P("dp", "tensor"),
        P("dp", "tensor"),
        P("dp", "tensor"),
        P("dp"),
        P(),
        P(),
        P(None, "tensor"),
        P(None, "tensor"),
        P("tensor", None),
    )
    out_specs = P("dp", "tensor")
    return jax.shard_map(body, mesh=mesh, in_specs=in_specs, out_specs=out_specs, check_vma=False)
```
